128 devices in a mesh: row: 8 (over y, z_lo), col: 16 (over z_hi, x, core).
Axes of the slice: x: 4, y: 4, z: 4 (z_hi: 2, z_lo: 2; z = z_hi * 2 + z_lo), core: 2. Of those that a mesh axis runs over, the one named last changes fastest.
Arguments:
- features: bfloat16 [32768, 512], P(('row', 'col')), may hold values from -6 to 6
- adj_values: bfloat16 [8, 16, 32, 256, 256], P('row', 'col'), may hold values from -0.0625 to 0.0625
- block_cells: int32 [8, 16, 32], P('row', 'col'), may hold values from 0 to 127, as said below
- block_counts: int32 [8, 16], P('row', 'col'), may hold values from 8 to 32, as said below
- w_first: bfloat16 [512, 512], replicated, may hold values from -0.25 to 0.25
- w_second: bfloat16 [512, 512], replicated, may hold values from -0.25 to 0.25
- cotangent: bfloat16 [32768, 512], P(('row', 'col')), may hold values from -6 to 6
Outputs:
- out_act: bfloat16 [32768, 512], P(('row', 'col'))
- grad_input: bfloat16 [32768, 512], P(('row', 'col'))
- grad_first: float32 [512, 512], replicated
- grad_second: float32 [512, 512], replicated
The draws below stay inside these ranges and needn't reach their ends.
Inputs may be any that keep to these rules, and one draw needn't show every extreme that they name: `block_cells`: within one tile the listed positions are distinct; each lies in 0 to 8 * 16 * 1^2 - 1. `block_counts`: some tile lists 32 live blocks.
All inputs are finite; a program needn't handle non-finite values.
Results may differ from the reference program's by a relative error of at most 0.034.
Values may be sent and summed in bfloat16 or wider, within the bound.
A program may use at most 128 MiB of HBM per device.

```python
import jax
import jax.numpy as jnp
from jax import lax

F = 512
NL = 256
BLK = 256
MAXB = 32
NODES = 32768
N_ROW = 8
N_COL = 16


def draw_block_cells(key, part):
    key = jax.random.fold_in(key, 11)
    total_cells = N_ROW * N_COL * (NL // BLK) * (NL // BLK)
    tile_keys = jax.random.split(key, N_ROW * N_COL)
    orders = jax.vmap(lambda one_key: jax.random.permutation(one_key, total_cells)[:MAXB])(tile_keys)
    return orders.reshape(N_ROW, N_COL, MAXB).astype(jnp.int32)


def draw_block_counts(key, part):
    key = jax.random.fold_in(key, 23)
    first_key, second_key, third_key = jax.random.split(key, 3)
    spread = MAXB - MAXB // 4
    first = jax.random.randint(first_key, (N_ROW * N_COL,), 0, spread + 1)
    second = jax.random.randint(second_key, (N_ROW * N_COL,), 0, spread + 1)
    counts = MAXB // 4 + first * second // spread
    chosen = jax.random.randint(third_key, (), 0, N_ROW * N_COL)
    counts = jnp.where(jnp.arange(N_ROW * N_COL) == chosen, MAXB, counts)
    return counts.reshape(N_ROW, N_COL).astype(jnp.int32)


def block_scale(key, extent, shards, low, largest):
    loudness, own = 1.0, jax.random.fold_in(key, 6)
    for position, parts in shards:
        heights = jnp.exp(jax.random.uniform(jax.random.fold_in(own, position), (parts,), jnp.float32, low / len(shards), largest / len(shards)))
        loudness = loudness * jnp.repeat(heights, extent[position] // parts).reshape([-1 if axis == position else 1 for axis in range(len(extent))])
    return loudness


def noise(stream_key, dims, width, most, pieces=(), kind=jnp.bfloat16):
    factor_of = block_scale(stream_key, dims, pieces, -0.22, 0.18) if pieces else 1.0
    values = jax.random.normal(stream_key, dims, jnp.float32) * width * factor_of
    return jnp.minimum(jnp.maximum(values, -most), most).astype(kind)


def setup_inputs(seed: int = 0) -> dict:
    splits = jax.random.split(jax.random.key(seed), 8)
    features = noise(splits[0], (NODES, F), 1.0, 6.0, ((0, 128),))
    adj_values = noise(splits[1], (N_ROW, N_COL, MAXB, BLK, BLK), (MAXB * BLK * BLK // NL) ** -0.5, 0.0625, ((0, 8), (1, 16)))
    block_cells = draw_block_cells(jax.random.fold_in(splits[7], 71), 0)
    block_counts = draw_block_counts(jax.random.fold_in(splits[7], 71), 0)
    w_first = noise(splits[4], (F, F), F ** -0.5, 0.25)
    w_second = noise(splits[5], (F, F), F ** -0.5, 0.25)
    cotangent = noise(splits[6], (NODES, F), 1.0, 6.0, ((0, 128),))
    return {"features": features, "adj_values": adj_values, "block_cells": block_cells, "block_counts": block_counts, "w_first": w_first, "w_second": w_second, "cotangent": cotangent}


def silu_slope(pre):
    sig = jax.nn.sigmoid(pre)
    return sig * (1.0 + pre * (1.0 - sig))


def tile_apply(values, cells, live_count, source, n_out, block_cols, transposed):
    rows_blk = cells // block_cols
    cols_blk = cells % block_cols
    if transposed:
        take_idx, put_idx = rows_blk, cols_blk
    else:
        take_idx, put_idx = cols_blk, rows_blk
    groups = values.shape[0] // 8

    def advance(group, total):
        begin = group * 8
        vals = lax.dynamic_slice_in_dim(values, begin, 8, 0).astype(jnp.float32)
        takes = lax.dynamic_slice_in_dim(take_idx, begin, 8, 0)
        puts = lax.dynamic_slice_in_dim(put_idx, begin, 8, 0)
        picked = jnp.take(source, takes, axis=0).astype(jnp.float32)
        if transposed:
            product = jnp.einsum('sab,saf->sbf', vals, picked)
        else:
            product = jnp.einsum('sab,sbf->saf', vals, picked)
        slot_ids = begin + jnp.arange(8, dtype=jnp.int32)
        onehot = ((jnp.arange(n_out, dtype=jnp.int32)[:, None] == puts[None, :]) & (slot_ids < live_count)[None, :]).astype(jnp.float32)
        return total + jnp.einsum('os,saf->oaf', onehot, product, precision=lax.Precision.HIGHEST)

    start = jnp.zeros((n_out, source.shape[1], source.shape[2]), jnp.float32)
    return lax.fori_loop(0, groups, advance, start)


def round_trip(partial_value):
    rounded = lax.optimization_barrier(partial_value.astype(jnp.bfloat16))
    return rounded.astype(jnp.float32)


def aggregate(source, adj_values, block_cells, block_counts):
    block_rows = N_COL * NL // BLK
    block_cols = N_ROW * NL // BLK
    grid = source.reshape(N_ROW, N_COL, NL, F)

    def one_group(row_index):
        def advance(total, col_index):
            colsrc = lax.dynamic_index_in_dim(grid, col_index, 1, keepdims=False).reshape(block_cols, BLK, F)
            vals = adj_values[row_index, col_index]
            partial_value = tile_apply(vals, block_cells[row_index, col_index], block_counts[row_index, col_index], colsrc, block_rows, block_cols, False)
            return total + round_trip(partial_value), None
        total, _ = lax.scan(advance, jnp.zeros((block_rows, BLK, F), jnp.float32), jnp.arange(N_COL, dtype=jnp.int32))
        return total

    result = lax.map(one_group, jnp.arange(N_ROW, dtype=jnp.int32))
    return result.reshape(N_ROW * N_COL * NL, F)


def aggregate_back(source, adj_values, block_cells, block_counts):
    block_rows = N_COL * NL // BLK
    block_cols = N_ROW * NL // BLK
    groups_src = source.reshape(N_ROW, block_rows, BLK, F)

    def one_group(col_index):
        def advance(total, row_index):
            rowsrc = lax.dynamic_index_in_dim(groups_src, row_index, 0, keepdims=False)
            vals = adj_values[row_index, col_index]
            partial_value = tile_apply(vals, block_cells[row_index, col_index], block_counts[row_index, col_index], rowsrc, block_cols, block_cols, True)
            return total + round_trip(partial_value), None
        total, _ = lax.scan(advance, jnp.zeros((block_cols, BLK, F), jnp.float32), jnp.arange(N_ROW, dtype=jnp.int32))
        return total

    result = lax.map(one_group, jnp.arange(N_COL, dtype=jnp.int32))
    result = result.reshape(N_COL, N_ROW, NL, F).transpose(1, 0, 2, 3)
    return result.reshape(N_ROW * N_COL * NL, F)


def reference(features, adj_values, block_cells, block_counts, w_first, w_second, cotangent):
    agg_first = aggregate(features, adj_values, block_cells, block_counts).astype(jnp.bfloat16)
    pre_first = jnp.dot(agg_first, w_first, preferred_element_type=jnp.float32)
    hidden = jax.nn.silu(pre_first).astype(jnp.bfloat16)
    agg_second = aggregate(hidden, adj_values, block_cells, block_counts).astype(jnp.bfloat16)
    pre_second = jnp.dot(agg_second, w_second, preferred_element_type=jnp.float32)
    out_act = jax.nn.silu(pre_second).astype(jnp.bfloat16)
    d_second = (cotangent.astype(jnp.float32) * silu_slope(pre_second)).astype(jnp.bfloat16)
    grad_second = lax.dot_general(agg_second, d_second, (((0,), (0,)), ((), ())), preferred_element_type=jnp.float32)
    back_second = lax.dot_general(d_second, w_second, (((1,), (1,)), ((), ())), preferred_element_type=jnp.float32).astype(jnp.bfloat16)
    d_hidden = aggregate_back(back_second, adj_values, block_cells, block_counts)
    d_first = (d_hidden * silu_slope(pre_first)).astype(jnp.bfloat16)
    grad_first = lax.dot_general(agg_first, d_first, (((0,), (0,)), ((), ())), preferred_element_type=jnp.float32)
    back_first = lax.dot_general(d_first, w_first, (((1,), (1,)), ((), ())), preferred_element_type=jnp.float32).astype(jnp.bfloat16)
    grad_input = aggregate_back(back_first, adj_values, block_cells, block_counts).astype(jnp.bfloat16)
    return (out_act, grad_input, grad_first, grad_second)
```

```python
import functools

import jax
import jax.numpy as jnp
from jax import lax
from jax.experimental import pallas as pl
from jax.experimental.pallas import tpu as pltpu
from jax.sharding import PartitionSpec as P

MESH = pl.DeviceIdType.MESH
BF = jnp.bfloat16
F32 = jnp.float32
N_SEM = 360


def slot_plan(cells, live_count, block_cols, n_out, transposed):
    n = cells.shape[0]
    ids = jnp.arange(n, dtype=jnp.int32)
    rows, cols = cells // block_cols, cells % block_cols
    take, put = (rows, cols) if transposed else (cols, rows)
    put = jnp.where(ids < live_count, put, n_out)
    key = put * n + ids
    rank = jnp.sum((key[None, :] < key[:, None]).astype(jnp.int32), axis=1)
    hot = (rank[None, :] == ids[:, None]).astype(jnp.int32)
    order = jnp.sum(hot * ids[None, :], axis=1)
    takes = jnp.sum(hot * take[None, :], axis=1)
    first = jnp.sum((put[None, :] == put[:, None]) & (ids[None, :] < ids[:, None]), axis=1) == 0
    keep = jnp.sum(hot * jnp.where(first, 0, 1)[None, :], axis=1)
    outs = jnp.arange(16, dtype=jnp.int32)
    here = jnp.sum((put[None, :] == outs[:, None]).astype(jnp.int32), axis=1)
    upto = jnp.sum((put[None, :] <= outs[:, None]).astype(jnp.int32), axis=1)
    last = jnp.where(here > 0, upto - 1, n)
    return jnp.concatenate([order, takes, keep, last])


class Ring:
    def __init__(self, ring, pair, slot, device):
        self.ring, self.pair = ring, pair
        self.slot_of, self.device_of = slot, device

    def at(self, dr, dp):
        return lax.rem(self.ring + dr, 4), (1 - self.pair) if dp else self.pair

    def slot(self, dr, dp, **kw):
        return self.slot_of(*self.at(dr, dp), **kw)

    def device(self, dr, dp):
        return self.device_of(*self.at(dr, dp))


class Net:
    def __init__(self, send_sems, recv_sems):
        self.send_sems, self.recv_sems = send_sems, recv_sems
        self.used = 0
        self.open = {}

    def send(self, src, dst, device, group):
        i = self.used
        self.used += 1
        copy = pltpu.make_async_remote_copy(
            src_ref=src,
            dst_ref=dst,
            send_sem=self.send_sems.at[i],
            recv_sem=self.recv_sems.at[i],
            device_id=device,
            device_id_type=MESH,
        )
        copy.start()
        self.open.setdefault(group, []).append(copy)
        return copy

    def drain(self, group):
        for copy in self.open.pop(group, []):
            copy.wait_send()


def gather(net, geo, x, partner=None):
    half = x.shape[1] // 2
    low, high = pl.ds(0, half), pl.ds(half, half)
    right, left, pair = geo.device(1, 0), geo.device(3, 0), geo.device(0, 1)
    shares = []

    def share(dr, dp):
        if partner is not None:
            ref = x.at[geo.slot(dr, dp)]
            shares.append(net.send(ref, ref, partner, "x"))

    def spread(dp):
        ref = x.at[geo.slot(0, dp)]
        return net.send(ref, ref, right, "x"), net.send(ref, ref, left, "x")

    def forward(dp, from_left, from_right):
        from_left.wait_recv()
        ref = x.at[geo.slot(3, dp), low]
        a = net.send(ref, ref, right, "x")
        share(3, dp)
        from_right.wait_recv()
        ref = x.at[geo.slot(1, dp), high]
        b = net.send(ref, ref, left, "x")
        share(1, dp)
        return a, b

    ref = x.at[geo.slot(0, 0)]
    across = net.send(ref, ref, pair, "x")
    own = spread(0)
    share(0, 0)
    yield
    far_own = forward(0, *own)
    yield
    across.wait_recv()
    other = spread(1)
    share(0, 1)
    yield
    far_other = forward(1, *other)
    yield
    for c in far_own:
        c.wait_recv()
    share(2, 0)
    for c in far_other:
        c.wait_recv()
    share(2, 1)
    for c in shares:
        c.wait_recv()
    yield


ORDER = ((2, 1), (1, 1), (3, 1), (2, 0), (1, 0), (3, 0), (0, 1), (0, 0))
GROUPS = ((0, 3), (3, 3), (6, 2))


def place(dr, dp):
    return ORDER.index((dr, dp))


def scatter(net, geo, pick, s, buf, group, done, partner=None, t=None, rc=None):
    ra, rb, rd, total = buf
    half = s.shape[1] // 2
    low, high = pl.ds(0, half), pl.ds(half, half)
    right, left, pair = geo.device(1, 0), geo.device(3, 0), geo.device(0, 1)
    net.drain(group)
    cores = []
    if partner is not None:
        for begin, count in GROUPS:
            for i in range(begin, begin + count):
                t[i] = pick(geo.slot(*ORDER[i], other=True))
            cores.append(net.send(t.at[pl.ds(begin, count)], rc.at[pl.ds(begin, count)], partner, group))
    for i in range(8):
        s[i] = pick(geo.slot(*ORDER[i]))
    if partner is not None:
        yield
    first, near = {}, {}
    for dp in (1, 0):
        if partner is not None:
            g = 0 if dp else 1
            cores[g].wait_recv()
            for i in range(GROUPS[g][0], sum(GROUPS[g])):
                s[i] = (s[i].astype(F32) + rc[i].astype(F32)).astype(BF)
        far, to_r, to_l = s.at[place(2, dp)], s.at[place(1, dp)], s.at[place(3, dp)]
        first[dp] = (
            net.send(far.at[low], ra.at[dp, 0], right, group),
            net.send(far.at[high], ra.at[dp, 1], left, group),
        )
        near[dp] = [
            net.send(to_r.at[high], rb.at[dp, 0, 1], right, group),
            net.send(to_l.at[low], rb.at[dp, 1, 0], left, group),
        ]
    if partner is not None:
        cores[2].wait_recv()
        for i in (6, 7):
            s[i] = (s[i].astype(F32) + rc[i].astype(F32)).astype(BF)
    yield
    for dp in (1, 0):
        to_r, to_l = place(1, dp), place(3, dp)
        first[dp][0].wait_recv()
        s[to_r, low] = (s[to_r, low].astype(F32) + ra[dp, 0].astype(F32)).astype(BF)
        near[dp].append(net.send(s.at[to_r, low], rb.at[dp, 0, 0], right, group))
        first[dp][1].wait_recv()
        s[to_l, high] = (s[to_l, high].astype(F32) + ra[dp, 1].astype(F32)).astype(BF)
        near[dp].append(net.send(s.at[to_l, high], rb.at[dp, 1, 1], left, group))
    yield

    def come(dp, h):
        rows = (low, high)[h]
        return s[place(0, dp), rows].astype(F32) + rb[dp, 0, h].astype(F32) + rb[dp, 1, h].astype(F32)

    for c in near[1]:
        c.wait_recv()
    for h in range(2):
        s[place(0, 1), (low, high)[h]] = come(1, h).astype(BF)
    last = net.send(s.at[place(0, 1)], rd, pair, group)
    yield
    for c in near[0]:
        c.wait_recv()
    for h in range(2):
        total[(low, high)[h]] = come(0, h)
    yield
    last.wait_recv()
    done(total[...] + rd[...].astype(F32))
    yield


def all_reduce(net, g, bufs, where, out):
    x, y, z, core, dev_x, dev_y, dev_z, partner = where
    b1, r1, h1, b2, r2, h2, b3, r3, h3, b4, r4, gb = bufs
    n = h1.shape[0]
    mine = pl.ds(pl.multiple_of(core * n, n), n)
    his = pl.ds(pl.multiple_of((1 - core) * n, n), n)
    b1[...] = g[his, :].astype(BF)
    c = net.send(b1, r1, partner, "g")
    yield
    c.wait_recv()
    h1[...] = g[mine, :] + r1[...].astype(F32)
    m = h2.shape[0]
    for k in range(4):
        b2[k] = h1[pl.ds(k * m, m), :].astype(BF)
    cs = [net.send(b2.at[lax.rem(x + d, 4)], r2.at[d - 1], dev_x(d), "g") for d in (1, 2, 3)]
    yield
    for c in cs:
        c.wait_recv()
    h2[...] = h1[pl.ds(pl.multiple_of(x * m, m), m), :] + r2[0].astype(F32) + r2[1].astype(F32) + r2[2].astype(F32)
    m = h3.shape[0]
    for k in range(4):
        b3[k] = h2[pl.ds(k * m, m), :].astype(BF)
    cs = [net.send(b3.at[lax.rem(y + d, 4)], r3.at[d - 1], dev_y(d), "g") for d in (1, 2, 3)]
    yield
    for c in cs:
        c.wait_recv()
    h3[...] = h2[pl.ds(pl.multiple_of(y * m, m), m), :] + r3[0].astype(F32) + r3[1].astype(F32) + r3[2].astype(F32)
    w = b4.shape[2]
    for k in range(4):
        b4[k] = h3[:, k * w : (k + 1) * w].astype(BF)
    cs = [net.send(b4.at[lax.rem(z + d, 4)], r4.at[d - 1], dev_z(d), "g") for d in (1, 2, 3)]
    yield
    for c in cs:
        c.wait_recv()
    piece = h3[:, pl.ds(pl.multiple_of(z * w, w), w)]
    piece = piece + r4[0].astype(F32) + r4[1].astype(F32) + r4[2].astype(F32)
    gb[core, x, y, z] = piece.astype(BF)
    ref = gb.at[core, x, y, z]
    cs = [net.send(ref, ref, dev_z(d), "g") for d in (1, 2, 3)]
    yield
    for c in cs:
        c.wait_recv()
    ref = gb.at[core, x, y]
    cs = [net.send(ref, ref, dev_y(d), "g") for d in (1, 2, 3)]
    yield
    for c in cs:
        c.wait_recv()
    ref = gb.at[core, x]
    cs = [net.send(ref, ref, dev_x(d), "g") for d in (1, 2, 3)]
    yield
    for c in cs:
        c.wait_recv()
    ref = gb.at[core]
    c = net.send(ref, ref, partner, "g")
    yield
    c.wait_recv()
    m = h3.shape[0]

    def write(i, carry):
        for k in range(4):
            begin = pl.multiple_of(i * m, m)
            out[pl.ds(begin, m), k * w : (k + 1) * w] = gb[i // 16, lax.rem(i // 4, 4), lax.rem(i, 4), k].astype(F32)
        return carry

    lax.fori_loop(0, 32, write, 0)
    yield


def slope(pre):
    sig = jax.nn.sigmoid(pre)
    return sig * (1.0 + pre * (1.0 - sig))


def dot_rows(a, b):
    return lax.dot_general(a, b, (((0,), (0,)), ((), ())), preferred_element_type=F32)


def dot_cols(a, b):
    return lax.dot_general(a, b, (((1,), (1,)), ((), ())), preferred_element_type=F32)


def dot(a, b):
    return jnp.dot(a, b, preferred_element_type=F32)


def kernel(names, plan, features, values_hbm, w_first, w_second, cotangent,
           out_act, grad_input, grad_first, grad_second, *scratch):
    m = dict(zip(names, scratch))
    row, col = lax.axis_index("row"), lax.axis_index("col")
    y, zl = row // 2, lax.rem(row, 2)
    zh, x, core = col // 8, lax.rem(col // 2, 4), lax.rem(col, 2)
    z = zh * 2 + zl

    def col_slot(r, p, other=False):
        return p * 8 + r * 2 + ((1 - core) if other else core)

    rows = Ring(y, zl, lambda r, p: r * 2 + p, lambda r, p: (r * 2 + p, col))
    cols = Ring(x, zh, col_slot, lambda r, p: (row, col_slot(r, p)))
    partner = (row, col_slot(x, zh, other=True))

    def dev_x(d):
        return cols.device(d, 0)

    def dev_y(d):
        return rows.device(d, 0)

    def dev_z(d):
        there = lax.rem(z + d, 4)
        return (y * 2 + lax.rem(there, 2), col_slot(x, there // 2))

    load = pltpu.make_async_copy(values_hbm, m["a"], m["load_sem"].at[0])
    load.start()

    barrier = pltpu.get_barrier_semaphore()
    peers = [f(d) for f in (dev_x, dev_y, dev_z) for d in (1, 2, 3)] + [partner]
    for peer in peers:
        pl.semaphore_signal(barrier, inc=1, device_id=peer, device_id_type=MESH)
    pl.semaphore_wait(barrier, len(peers))

    net = Net(m["send_sems"], m["recv_sems"])
    nl, width = features.shape
    wc = width // 2
    chunk = [slice(0, wc), slice(wc, width)]
    n_slots = m["a"].shape[0]
    prod, acc = m["prod"], m["acc"]

    def tile(a, xc, base):
        acc[...] = jnp.zeros_like(acc)

        def step(i, carry):
            p = dot(a[plan[base + i]], xc[plan[base + n_slots + i]])
            v = jnp.where(plan[base + 2 * n_slots + i] > 0, acc[...], 0.0) + p
            acc[...] = v
            prod[i] = v.astype(BF)
            return carry

        lax.fori_loop(0, n_slots, step, 0, unroll=2)

    prod[n_slots] = jnp.zeros(prod.shape[1:], BF)
    reduces = [None, None]

    def side(k, steps=1):
        if reduces[k] is not None:
            for _ in range(steps):
                next(reduces[k], None)

    def aggregate(name, back, ag, start_second, filler, done):
        a = m["at"] if back else m["a"]
        base = 3 * n_slots + 16 if back else 0
        geo = rows if back else cols

        def pick(slot):
            return prod[plan[base + 3 * n_slots + slot]]

        extra = (lambda c: {}) if back else (
            lambda c: {"partner": partner, "t": m["t", c], "rc": m["rc", name, c]}
        )
        rs = [
            scatter(
                net, geo, pick, m["s", c],
                (m["ra", name, c], m["rb", name, c], m["rd", name, c], m["total", c]),
                ("s", c), functools.partial(done, c), **extra(c),
            )
            for c in range(2)
        ]
        next(ag[0])
        start_second()
        next(ag[0])
        next(ag[0])
        next(ag[1])
        next(ag[0])
        filler()
        next(ag[0])
        tile(a, m["x", name, 0], base)
        next(rs[0])
        side(0)
        next(ag[1])
        next(ag[1])
        if not back:
            next(rs[0])
        next(ag[1])
        side(0)
        next(rs[0])
        next(ag[1])
        side(0)
        tile(a, m["x", name, 1], base)
        next(rs[1])
        next(rs[0])
        if not back:
            next(rs[1])
        side(0)
        next(rs[0])
        next(rs[1])
        side(0)
        next(rs[0])
        next(rs[1])
        side(0)
        next(rs[1])
        next(rs[1])

    def gathers(name, back):
        geo, other = (cols, partner) if back else (rows, None)
        return [gather(net, geo, m["x", name, c], other) for c in range(2)]

    agg, pre_first, pre_second, d_second, d_first = (m[k] for k in ("agg", "pre1", "pre2", "d2", "d1"))

    def own_f(name, c, value):
        m["x", name, c][rows.slot(0, 0)] = value.astype(BF)

    def own_b(name, c, value):
        m["x", name, c][cols.slot(0, 0)] = value.astype(BF)

    def layer(k, pre, w):
        def done(c, value):
            agg[k, c] = value.astype(BF)
            if c == 0:
                pre[...] = dot(agg[k, 0], w[0:wc, :])
            else:
                for n in range(2):
                    pre[:, chunk[n]] += dot(agg[k, 1], w[wc:width, chunk[n]])
                    after[k](n)
        return done

    def hidden(n):
        if n == 0:
            own_f("f2", 0, jax.nn.silu(pre_first[:, chunk[0]]))

    def output(n):
        u = pre_second[:, chunk[n]]
        out_act[:, chunk[n]] = jax.nn.silu(u).astype(BF)
        d_second[:, chunk[n]] = (cotangent[:, chunk[n]].astype(F32) * slope(u)).astype(BF)

    after = [hidden, output]

    own_f("f1", 0, features[:, chunk[0]])
    aggregate(
        "f1", False, gathers("f1", False),
        lambda: own_f("f1", 1, features[:, chunk[1]]), load.wait, layer(0, pre_first, w_first),
    )

    def turn():
        def one(i, carry):
            m["at"][i] = m["a"][i].T
            return carry
        lax.fori_loop(0, n_slots, one, 0)

    aggregate(
        "f2", False, gathers("f2", False),
        lambda: own_f("f2", 1, jax.nn.silu(pre_first[:, chunk[1]])), turn, layer(1, pre_second, w_second),
    )

    where = (x, y, z, core, dev_x, dev_y, dev_z, partner)

    def weight_grad(k, d, out, name):
        for c in range(2):
            out[chunk[c], :] = dot_rows(agg[k, c], d[...])
        bufs = [m[key, name] for key in AR_KEYS]
        g = all_reduce(net, out, bufs, where, out)
        next(g)
        return g

    def start_grad(slot, k, d, out, name):
        def run():
            reduces[slot] = weight_grad(k, d, out, name)
        return run

    def hidden_back(c, value):
        d_first[:, chunk[c]] = (value * slope(pre_first[:, chunk[c]])).astype(BF)

    own_b("b2", 0, dot_cols(d_second[...], w_second[chunk[0], :]))
    aggregate(
        "b2", True, gathers("b2", True),
        lambda: own_b("b2", 1, dot_cols(d_second[...], w_second[chunk[1], :])),
        start_grad(0, 1, d_second, grad_second, "g2"), hidden_back,
    )
    side(0, 20)

    def input_back(c, value):
        grad_input[:, chunk[c]] = value.astype(BF)

    own_b("b1", 0, dot_cols(d_first[...], w_first[chunk[0], :]))
    aggregate(
        "b1", True, gathers("b1", True),
        lambda: own_b("b1", 1, dot_cols(d_first[...], w_first[chunk[1], :])),
        start_grad(0, 0, d_first, grad_first, "g1"), input_back,
    )
    side(0, 20)
    for group in list(net.open):
        net.drain(group)


AR_KEYS = ("b1", "r1", "h1", "b2", "r2", "h2", "b3", "r3", "h3", "b4", "r4", "gb")


def scratch_of(nl, width, side, slots):
    w = width // 2
    s = {}

    def add(key, shape, kind=BF):
        s[key] = pltpu.VMEM(shape, kind)

    add("a", (slots, side, side))
    add("at", (slots, side, side))
    add("prod", (slots + 1, side, w))
    add("acc", (side, w), F32)
    for c in range(2):
        add(("s", c), (8, nl, w))
        add(("t", c), (8, nl, w))
        add(("total", c), (nl, w), F32)
        for name, blocks in (("f1", 8), ("f2", 8), ("b2", 16), ("b1", 16)):
            add(("x", name, c), (blocks, nl, w))
            add(("ra", name, c), (2, 2, nl // 2, w))
            add(("rb", name, c), (2, 2, 2, nl // 2, w))
            add(("rd", name, c), (nl, w))
            if blocks == 8:
                add(("rc", name, c), (8, nl, w))
    add("agg", (2, 2, nl, w))
    add("pre1", (nl, width), F32)
    add("pre2", (nl, width), F32)
    add("d2", (nl, width))
    add("d1", (nl, width))
    h = width
    for name in ("g2", "g1"):
        add(("b1", name), (h // 2, width))
        add(("r1", name), (h // 2, width))
        add(("h1", name), (h // 2, width), F32)
        add(("b2", name), (4, h // 8, width))
        add(("r2", name), (3, h // 8, width))
        add(("h2", name), (h // 8, width), F32)
        add(("b3", name), (4, h // 32, width))
        add(("r3", name), (3, h // 32, width))
        add(("h3", name), (h // 32, width), F32)
        add(("b4", name), (4, h // 32, width // 4))
        add(("r4", name), (3, h // 32, width // 4))
        add(("gb", name), (2, 4, 4, 4, h // 32, width // 4))
    s["load_sem"] = pltpu.SemaphoreType.DMA((1,))
    s["send_sems"] = pltpu.SemaphoreType.DMA((N_SEM,))
    s["recv_sems"] = pltpu.SemaphoreType.DMA((N_SEM,))
    return s


def local(features, adj_values, block_cells, block_counts, w_first, w_second, cotangent):
    values, cells, live = adj_values[0, 0], block_cells[0, 0], block_counts[0, 0]
    nl, width = features.shape
    slots, side, _ = values.shape
    plan = jnp.concatenate([slot_plan(cells, live, 8, 16, False), slot_plan(cells, live, 8, 8, True)])
    scratch = scratch_of(nl, width, side, slots)
    vmem = pl.BlockSpec(memory_space=pltpu.VMEM)
    return pl.pallas_call(
        functools.partial(kernel, tuple(scratch)),
        out_shape=(
            jax.ShapeDtypeStruct((nl, width), BF),
            jax.ShapeDtypeStruct((nl, width), BF),
            jax.ShapeDtypeStruct((width, width), F32),
            jax.ShapeDtypeStruct((width, width), F32),
        ),
        in_specs=[pl.BlockSpec(memory_space=pltpu.SMEM), vmem, pl.BlockSpec(memory_space=pl.ANY), vmem, vmem, vmem],
        out_specs=(vmem, vmem, vmem, vmem),
        scratch_shapes=list(scratch.values()),
        compiler_params=pltpu.CompilerParams(
            collective_id=0, has_side_effects=True, vmem_limit_bytes=63 * 1024 * 1024 - 512 * 1024
        ),
    )(plan, features, values, w_first, w_second, cotangent)


def solution(mesh):
    return jax.shard_map(
        local,
        mesh=mesh,
        in_specs=(
            P(("row", "col"), None),
            P("row", "col", None, None, None),
            P("row", "col", None),
            P("row", "col"),
            P(),
            P(),
            P(("row", "col"), None),
        ),
        out_specs=(P(("row", "col"), None), P(("row", "col"), None), P(), P()),
        check_vma=False,
    )
```

```python
import functools

import jax
import jax.numpy as jnp
from jax import lax
from jax.experimental import pallas as pl
from jax.experimental.pallas import tpu as pltpu
from jax.sharding import PartitionSpec as P

MESH = pl.DeviceIdType.MESH
BF = jnp.bfloat16
F32 = jnp.float32


def slot_plan(cells, live_count, block_cols, n_out, transposed):
    n = cells.shape[0]
    ids = jnp.arange(n, dtype=jnp.int32)
    rows, cols = cells // block_cols, cells % block_cols
    take, put = (rows, cols) if transposed else (cols, rows)
    put = jnp.where(ids < live_count, put, n_out)
    key = put * n + ids
    rank = jnp.sum((key[None, :] < key[:, None]).astype(jnp.int32), axis=1)
    hot = (rank[None, :] == ids[:, None]).astype(jnp.int32)
    order = jnp.sum(hot * ids[None, :], axis=1)
    takes = jnp.sum(hot * take[None, :], axis=1)
    first = jnp.sum((put[None, :] == put[:, None]) & (ids[None, :] < ids[:, None]), axis=1) == 0
    keep = jnp.sum(hot * jnp.where(first, 0, 1)[None, :], axis=1)
    outs = jnp.arange(16, dtype=jnp.int32)
    here = jnp.sum((put[None, :] == outs[:, None]).astype(jnp.int32), axis=1)
    upto = jnp.sum((put[None, :] <= outs[:, None]).astype(jnp.int32), axis=1)
    last = jnp.where(here > 0, upto - 1, n)
    return jnp.concatenate([order, takes, keep, last])


class Ring:
    def __init__(self, ring, pair, slot, device):
        self.ring, self.pair = ring, pair
        self.slot_of, self.device_of = slot, device

    def at(self, dr, dp):
        return lax.rem(self.ring + dr, 4), (1 - self.pair) if dp else self.pair

    def slot(self, dr, dp, **kw):
        return self.slot_of(*self.at(dr, dp), **kw)

    def device(self, dr, dp):
        return self.device_of(*self.at(dr, dp))


class Net:
    def __init__(self, send_sems, recv_sems):
        self.send_sems, self.recv_sems = send_sems, recv_sems
        self.names, self.sends = {}, {}
        self.open = {}

    def send(self, src, dst, device, group, name):
        i = self.names.setdefault(name, len(self.names))
        now = self.open.setdefault(group, [])
        j = self.sends.setdefault((group, len(now)), len(self.sends))
        copy = pltpu.make_async_remote_copy(
            src_ref=src,
            dst_ref=dst,
            send_sem=self.send_sems.at[j],
            recv_sem=self.recv_sems.at[i],
            device_id=device,
            device_id_type=MESH,
        )
        copy.start()
        now.append(copy)
        return copy

    def arrived(self, ref, device, name):
        pltpu.make_async_remote_copy(
            src_ref=ref,
            dst_ref=ref,
            send_sem=self.send_sems.at[0],
            recv_sem=self.recv_sems.at[self.names[name]],
            device_id=device,
            device_id_type=MESH,
        ).wait_recv()

    def drain(self, group):
        for copy in self.open.pop(group, []):
            copy.wait_send()


def gather(net, geo, x, key, group, direct, partner=None):
    half = x.shape[1] // 2
    low, high = pl.ds(0, half), pl.ds(half, half)
    right, left, pair, far = geo.device(1, 0), geo.device(3, 0), geo.device(0, 1), geo.device(2, 0)
    net.drain(group)

    def send(ref, device, name):
        return net.send(ref, ref, device, group, (key, name))

    def share(dr, dp):
        if partner is not None:
            send(x.at[geo.slot(dr, dp)], partner, "share")

    mine, his = x.at[geo.slot(0, 0)], x.at[geo.slot(0, 1)]
    across = send(mine, pair, "across")
    own_r, own_l = send(mine, right, "own_r"), send(mine, left, "own_l")
    share(0, 0)
    yield
    own_r.wait_recv()
    far_a = send(x.at[geo.slot(3, 0), low], right, "far_a")
    own_l.wait_recv()
    far_b = send(x.at[geo.slot(1, 0), high], left, "far_b")
    share(3, 0)
    share(1, 0)
    yield
    across.wait_recv()
    other = [send(his, right, "other_r"), send(his, left, "other_l")]
    if direct:
        other.append(send(his, far, "other_f"))
    share(0, 1)
    yield
    far_a.wait_recv()
    far_b.wait_recv()
    if not direct:
        other.append(send(x.at[geo.slot(2, 0)], pair, "other_f"))
    share(2, 0)
    yield
    for c, dr in zip(other, (3, 1, 2)):
        c.wait_recv()
        share(dr, 1)
    yield
    if partner is not None:
        net.arrived(x.at[pl.ds(0, 8)], partner, (key, "share"))
    yield


ORDER = ((2, 1), (1, 1), (3, 1), (1, 0), (3, 0), (2, 0), (0, 1), (0, 0))
GROUPS = ((0, 1), (1, 4), (5, 1), (6, 2))


def place(dr, dp):
    return ORDER.index((dr, dp))


def scatter(net, geo, pick, s, buf, key, group, done, direct, partner=None, t=None, rc=None):
    ra, rp, rq, rd, total = buf
    half = s.shape[1] // 2
    low, high = pl.ds(0, half), pl.ds(half, half)
    right, left, pair, far = geo.device(1, 0), geo.device(3, 0), geo.device(0, 1), geo.device(2, 0)
    net.drain(group)

    def send(src, dst, device, name):
        return net.send(src, dst, device, group, (key, name))

    cores = []
    if partner is not None:
        for g, (begin, count) in enumerate(GROUPS):
            for i in range(begin, begin + count):
                t[i] = pick(geo.slot(*ORDER[i], other=True))
            there = pl.ds(begin, count)
            cores.append(send(t.at[there], rc.at[there], partner, ("core", g)))

    def bring(g):
        for i in range(GROUPS[g][0], sum(GROUPS[g])):
            s[i] = pick(geo.slot(*ORDER[i]))

    def add(g):
        if partner is not None:
            cores[g].wait_recv()
            for i in range(GROUPS[g][0], sum(GROUPS[g])):
                s[i] = (s[i].astype(F32) + rc[i].astype(F32)).astype(BF)

    def send_other():
        if direct:
            send(s.at[place(2, 1)], rq.at[2], far, "q")
        else:
            send(s.at[place(2, 1)], rq.at[2], pair, "far")

    def send_near():
        send(s.at[place(1, 1)], rq.at[0], right, "q")
        send(s.at[place(3, 1)], rq.at[1], left, "q")
        send(s.at[place(1, 0), high], rp.at[0, 1], right, "p")
        send(s.at[place(3, 0), low], rp.at[1, 0], left, "p")

    def send_far():
        i = place(2, 0)
        if not direct:
            net.arrived(rq.at[2], pair, (key, "far"))
            s[i] = (s[i].astype(F32) + rq[2].astype(F32)).astype(BF)
        return send(s.at[i, low], ra.at[0], right, "a"), send(s.at[i, high], ra.at[1], left, "b")

    if partner is None:
        bring(0)
        send_other()
        bring(1)
        send_near()
        bring(2)
        bring(3)
        yield
        yield
        first = send_far()
    else:
        for g in range(4):
            bring(g)
        yield
        add(0)
        send_other()
        add(1)
        send_near()
        yield
        add(2)
        first = send_far()
        add(3)
    yield
    i = place(0, 1)
    if direct:
        net.arrived(rq, pair, (key, "q"))
        s[i] = (s[i].astype(F32) + rq[0].astype(F32) + rq[1].astype(F32) + rq[2].astype(F32)).astype(BF)
    else:
        net.arrived(rq.at[pl.ds(0, 2)], pair, (key, "q"))
        s[i] = (s[i].astype(F32) + rq[0].astype(F32) + rq[1].astype(F32)).astype(BF)
    last = send(s.at[i], rd, pair, "last")
    yield
    to_r, to_l = place(1, 0), place(3, 0)
    first[0].wait_recv()
    s[to_r, low] = (s[to_r, low].astype(F32) + ra[0].astype(F32)).astype(BF)
    send(s.at[to_r, low], rp.at[0, 0], right, "p")
    first[1].wait_recv()
    s[to_l, high] = (s[to_l, high].astype(F32) + ra[1].astype(F32)).astype(BF)
    send(s.at[to_l, high], rp.at[1, 1], left, "p")
    yield
    net.arrived(rp, pair, (key, "p"))
    for h, rows in enumerate((low, high)):
        total[rows] = s[place(0, 0), rows].astype(F32) + rp[0, h].astype(F32) + rp[1, h].astype(F32)
    yield
    last.wait_recv()
    done(total[...] + rd[...].astype(F32))
    yield


def all_reduce(net, g, bufs, where, out, key):
    x, y, z, core, dev_x, dev_yz, partner = where
    b1, r1, h1, b2, r2, h2, b3, r3, gb = bufs
    n, m, w = h1.shape[0], h2.shape[0], b3.shape[2]
    plane = [(dy, dz) for dy in range(4) for dz in range(4) if (dy, dz) != (0, 0)]
    here = y * 4 + z

    def there(dy, dz):
        return lax.rem(y + dy, 4) * 4 + lax.rem(z + dz, 4)

    mine = pl.ds(pl.multiple_of(core * n, n), n)
    his = pl.ds(pl.multiple_of((1 - core) * n, n), n)
    b1[...] = g[his, :].astype(BF)
    c = net.send(b1, r1, partner, "g", (key, 1))
    yield
    c.wait_recv()
    h1[...] = g[mine, :] + r1[...].astype(F32)
    for k in range(16):
        b2[k] = h1[k * m : (k + 1) * m, :].astype(BF)
    for k, d in enumerate(plane):
        net.send(b2.at[there(*d)], r2.at[k], dev_yz(*d), "g", (key, 2))
    yield
    net.arrived(r2, partner, (key, 2))
    total = h1[pl.ds(pl.multiple_of(here * m, m), m), :]
    for k in range(15):
        total = total + r2[k].astype(F32)
    h2[...] = total
    for k in range(4):
        b3[k] = h2[:, k * w : (k + 1) * w].astype(BF)
    for d in (1, 2, 3):
        net.send(b3.at[lax.rem(x + d, 4)], r3.at[d - 1], dev_x(d), "g", (key, 3))
    yield
    net.arrived(r3, partner, (key, 3))
    piece = h2[:, pl.ds(pl.multiple_of(x * w, w), w)]
    piece = piece + r3[0].astype(F32) + r3[1].astype(F32) + r3[2].astype(F32)
    gb[core, here, x] = piece.astype(BF)
    ref = gb.at[core, here, x]
    for d in (1, 2, 3):
        net.send(ref, ref, dev_x(d), "g", (key, 4))
    yield
    net.arrived(gb.at[0, 0, pl.ds(0, 3)], partner, (key, 4))
    ref_p = gb.at[core, here]
    for d in plane:
        net.send(ref_p, ref_p, dev_yz(*d), "g", (key, 5))
    yield
    net.arrived(gb.at[0, pl.ds(0, 15)], partner, (key, 5))
    ref_c = gb.at[core]
    c = net.send(ref_c, ref_c, partner, "g", (key, 6))
    yield
    c.wait_recv()

    def write(i, carry):
        for k in range(4):
            begin = pl.multiple_of(i * m, m)
            out[pl.ds(begin, m), k * w : (k + 1) * w] = gb[i // 16, lax.rem(i, 16), k]
        return carry

    lax.fori_loop(0, 32, write, 0, unroll=4)
    yield


def slope(pre):
    sig = jax.nn.sigmoid(pre)
    return sig * (1.0 + pre * (1.0 - sig))


def dot_rows(a, b):
    return lax.dot_general(a, b, (((0,), (0,)), ((), ())), preferred_element_type=F32)


def dot_cols(a, b):
    return lax.dot_general(a, b, (((1,), (1,)), ((), ())), preferred_element_type=F32)


def dot(a, b):
    return jnp.dot(a, b, preferred_element_type=F32)


WIDTHS = (256, 256)
PROGRAM = (
    "O0", "O1", "F", "H0", "Q0", "S", "H1", "K0", "Q1", "E0", "K1", "G0", "S", "T0", "P0", "U0", "E1", "G1",
    "T1", "P1", "S", "V0", "U1", "V1", "C0", "B0", "S", "D0", "C1", "B1", "Z0", "S", "D1", "S", "Z1",
)
GATHER_DIRECT = (False, False)
SCATTER_DIRECT = (False, False)
SETS = {"f1": 0, "f2": 1, "b2": 0, "b1": 1}
UNROLL = 8


def kernel(names, plan, features, values_hbm, w_first_hbm, w_second_hbm, cotangent_hbm,
           out_act, grad_input, grad_first, grad_second, *scratch):
    m = dict(zip(names, scratch))
    row, col = lax.axis_index("row"), lax.axis_index("col")
    y, zl = row // 2, lax.rem(row, 2)
    zh, x, core = col // 8, lax.rem(col // 2, 4), lax.rem(col, 2)
    z = zh * 2 + zl

    def col_slot(r, p, other=False):
        return p * 8 + r * 2 + ((1 - core) if other else core)

    rows = Ring(y, zl, lambda r, p: r * 2 + p, lambda r, p: (r * 2 + p, col))
    cols = Ring(x, zh, col_slot, lambda r, p: (row, col_slot(r, p)))
    partner = (row, col_slot(x, zh, other=True))

    def dev_x(d):
        return cols.device(d, 0)

    def dev_yz(dy, dz):
        there = lax.rem(z + dz, 4)
        return (lax.rem(y + dy, 4) * 2 + lax.rem(there, 2), col_slot(x, there // 2))

    w_first, w_second, cotangent = m["w1"], m["w2"], m["cot"]
    loads = [
        pltpu.make_async_copy(src, dst, m["load_sems"].at[i])
        for i, (src, dst) in enumerate(
            ((values_hbm, m["a"]), (w_first_hbm, w_first), (w_second_hbm, w_second), (cotangent_hbm, cotangent))
        )
    ]

    barrier = pltpu.get_barrier_semaphore()
    peers = [dev_x(d) for d in (1, 2, 3)] + [partner]
    peers += [dev_yz(dy, dz) for dy in range(4) for dz in range(4) if (dy, dz) != (0, 0)]
    for peer in peers:
        pl.semaphore_signal(barrier, inc=1, device_id=peer, device_id_type=MESH)
    for load in loads:
        load.start()

    net = Net(m["send_sems"], m["recv_sems"])
    nl, width = features.shape
    chunks, begin = [], 0
    for w in WIDTHS:
        chunks.append(slice(begin, begin + w))
        begin += w
    n_chunks = len(chunks)
    n_slots = m["a"].shape[0]
    for w in sorted(set(WIDTHS)):
        prod = m["prod", w]
        prod[n_slots] = jnp.zeros(prod.shape[1:], BF)

    def tile(a, xc, base, w):
        prod, acc = m["prod", w], m["acc", w]
        acc[...] = jnp.zeros_like(acc)

        def step(i, carry):
            p = dot(a[plan[base + i]], xc[plan[base + n_slots + i]])
            v = jnp.where(plan[base + 2 * n_slots + i] > 0, acc[...], 0.0) + p
            acc[...] = v
            prod[i] = v.astype(BF)
            return carry

        lax.fori_loop(0, n_slots, step, 0, unroll=UNROLL)

    reduces = []

    def side(steps=1):
        for _ in range(steps):
            for g in reduces:
                next(g, None)

    def aggregate(name, back, own, filler, done):
        a = m["at"] if back else m["a"]
        base = 3 * n_slots + 16 if back else 0
        geo_in, geo_out = (cols, rows) if back else (rows, cols)
        k = SETS[name]
        ag, rs = [], []
        for c, w in enumerate(WIDTHS):
            def pick(slot, prod=m["prod", w]):
                return prod[plan[base + 3 * n_slots + slot]]

            ag.append(
                gather(net, geo_in, m["x", name, c], ("x", k, c), ("x", c), GATHER_DIRECT[c], partner if back else None)
            )
            more = {} if back else {"partner": partner, "t": m["t", c], "rc": m["rc", name, c]}
            bufs = tuple(m[q, name, c] for q in ("ra", "rp", "rq", "rd")) + (m["total", c],)
            rs.append(
                scatter(
                    net, geo_out, pick, m["s", c], bufs, ("s", k, c), ("s", c),
                    functools.partial(done, c), SCATTER_DIRECT[c], **more,
                )
            )
        for word in PROGRAM:
            c = int(word[1:] or 0)
            if word[0] == "O":
                m["x", name, c][geo_in.slot(0, 0)] = own(c).astype(BF)
                if name == "f1" and c == 0:
                    pl.semaphore_wait(barrier, len(peers))
                next(ag[c])
            elif word[0] in "HQKEG":
                next(ag[c])
            elif word[0] == "T":
                tile(a, m["x", name, c], base, WIDTHS[c])
            elif word[0] == "S":
                side()
            elif word[0] == "F":
                filler()
            else:
                next(rs[c])

    agg, pre_first, pre_second, d_second, d_first = (m[q] for q in ("agg", "pre1", "pre2", "d2", "d1"))

    def layer(k, pre, w):
        def done(c, value):
            agg[k, :, chunks[c]] = value.astype(BF)
            part = dot(agg[k, :, chunks[c]], w[chunks[c], :])
            pre[...] = part if c == 0 else pre[...] + part

        return done

    def wait_loads():
        for load in loads:
            load.wait()

    aggregate("f1", False, lambda c: features[:, chunks[c]], wait_loads, layer(0, pre_first, w_first))

    def turn():
        def one(i, carry):
            m["at"][i] = m["a"][i].T
            return carry

        lax.fori_loop(0, n_slots, one, 0)

    aggregate(
        "f2", False, lambda c: jax.nn.silu(pre_first[:, chunks[c]]), turn, layer(1, pre_second, w_second)
    )
    for c in chunks:
        u = pre_second[:, c]
        d_second[:, c] = (cotangent[:, c].astype(F32) * slope(u)).astype(BF)

    where = (x, y, z, core, dev_x, dev_yz, partner)

    def weight_grad(k, d, out, name):
        g = m["grad", name]
        half = width // 2
        for c in (slice(0, half), slice(half, width)):
            g[c, :] = dot_rows(agg[k, :, c], d[...])
        reduces.append(all_reduce(net, g, [m[q, name] for q in AR_KEYS], where, out, ("g", name)))
        side()

    def hidden_back(c, value):
        d_first[:, chunks[c]] = (value * slope(pre_first[:, chunks[c]])).astype(BF)

    def second_grad():
        out_act[...] = jax.nn.silu(pre_second[...]).astype(BF)
        weight_grad(1, d_second, grad_second, "g2")

    aggregate("b2", True, lambda c: dot_cols(d_second[...], w_second[chunks[c], :]), second_grad, hidden_back)

    def input_back(c, value):
        grad_input[:, chunks[c]] = value.astype(BF)

    aggregate(
        "b1", True, lambda c: dot_cols(d_first[...], w_first[chunks[c], :]),
        lambda: weight_grad(0, d_first, grad_first, "g1"), input_back,
    )
    side(12)
    for group in list(net.open):
        net.drain(group)


AR_KEYS = ("b1", "r1", "h1", "b2", "r2", "h2", "b3", "r3", "gb")


def scratch_of(nl, width, side, slots):
    s = {}

    def add(key, shape, kind=BF):
        s[key] = pltpu.VMEM(shape, kind)

    add("a", (slots, side, side))
    add("at", (slots, side, side))
    add("w1", (width, width))
    add("w2", (width, width))
    add("cot", (nl, width))
    for w in sorted(set(WIDTHS)):
        add(("prod", w), (slots + 1, side, w))
        add(("acc", w), (side, w), F32)
    for c, w in enumerate(WIDTHS):
        add(("s", c), (8, nl, w))
        add(("t", c), (8, nl, w))
        add(("total", c), (nl, w), F32)
        for name, blocks in (("f1", 8), ("f2", 8), ("b2", 16), ("b1", 16)):
            add(("x", name, c), (blocks, nl, w))
            add(("ra", name, c), (2, nl // 2, w))
            add(("rp", name, c), (2, 2, nl // 2, w))
            add(("rq", name, c), (3, nl, w))
            add(("rd", name, c), (nl, w))
            if blocks == 8:
                add(("rc", name, c), (8, nl, w))
    add("agg", (2, nl, width))
    add("pre1", (nl, width), F32)
    add("pre2", (nl, width), F32)
    add("d2", (nl, width))
    add("d1", (nl, width))
    h = width
    for name in ("g2", "g1"):
        add(("grad", name), (width, width), F32)
        add(("b1", name), (h // 2, width))
        add(("r1", name), (h // 2, width))
        add(("h1", name), (h // 2, width), F32)
        add(("b2", name), (16, h // 32, width))
        add(("r2", name), (15, h // 32, width))
        add(("h2", name), (h // 32, width), F32)
        add(("b3", name), (4, h // 32, width // 4))
        add(("r3", name), (3, h // 32, width // 4))
        add(("gb", name), (2, 16, 4, h // 32, width // 4))
    s["load_sems"] = pltpu.SemaphoreType.DMA((4,))
    n = len(WIDTHS)
    s["send_sems"] = pltpu.SemaphoreType.DMA((30 * n + 76,))
    s["recv_sems"] = pltpu.SemaphoreType.DMA((38 * n + 14,))
    return s


def tail(out_act, grad_input, grad_first, grad_second, out_act_t, grad_input_t, grad_first_t, grad_second_t):
    out_act_t[...] = out_act[...]
    grad_input_t[...] = grad_input[...]
    grad_first_t[...] = grad_first[...].astype(F32)
    grad_second_t[...] = grad_second[...].astype(F32)


def local(features, adj_values, block_cells, block_counts, w_first, w_second, cotangent):
    values, cells, live = adj_values[0, 0], block_cells[0, 0], block_counts[0, 0]
    nl, width = features.shape
    slots, side, _ = values.shape
    plan = jnp.concatenate([slot_plan(cells, live, 8, 16, False), slot_plan(cells, live, 8, 8, True)])
    scratch = scratch_of(nl, width, side, slots)
    vmem = pl.BlockSpec(memory_space=pltpu.VMEM)
    hbm = pl.BlockSpec(memory_space=pl.ANY)

    def shapes(kind):
        node, weight = jax.ShapeDtypeStruct((nl, width), BF), jax.ShapeDtypeStruct((width, width), kind)
        return (node, node, weight, weight)

    outs = pl.pallas_call(
        functools.partial(kernel, tuple(scratch)),
        out_shape=shapes(BF),
        in_specs=[pl.BlockSpec(memory_space=pltpu.SMEM), vmem, hbm, hbm, hbm, hbm],
        out_specs=(vmem, vmem, vmem, vmem),
        scratch_shapes=list(scratch.values()),
        compiler_params=pltpu.CompilerParams(
            collective_id=0, has_side_effects=True, vmem_limit_bytes=63 * 1024 * 1024 - 512 * 1024
        ),
    )(plan, features, values, w_first, w_second, cotangent)
    return pl.pallas_call(
        tail,
        out_shape=shapes(F32),
        in_specs=[vmem] * 4,
        out_specs=(vmem,) * 4,
        compiler_params=pltpu.CompilerParams(vmem_limit_bytes=16 * 1024 * 1024),
    )(*outs)


def solution(mesh):
    return jax.shard_map(
        local,
        mesh=mesh,
        in_specs=(
            P(("row", "col"), None),
            P("row", "col", None, None, None),
            P("row", "col", None),
            P("row", "col"),
            P(),
            P(),
            P(("row", "col"), None),
        ),
        out_specs=(P(("row", "col"), None), P(("row", "col"), None), P(), P()),
        check_vma=False,
    )
```

```python
import functools

import jax
import jax.numpy as jnp
from jax import lax
from jax.experimental import pallas as pl
from jax.experimental.pallas import tpu as pltpu
from jax.sharding import PartitionSpec as P

MESH = pl.DeviceIdType.MESH
BF = jnp.bfloat16
F32 = jnp.float32


def slot_plan(cells, live, out, base, n_out, transposed):
    n = cells.shape[1]
    lane = lax.broadcasted_iota(jnp.int32, (n, n), 1)
    line = lax.broadcasted_iota(jnp.int32, (n, n), 0)
    cell = jnp.broadcast_to(cells[...], (n, n))

    def column(a):
        return jnp.sum(jnp.where(lane == line, a, 0), axis=1, keepdims=True)

    def line_sum(where, a):
        return jnp.sum(jnp.where(where, a, 0), axis=0, keepdims=True)

    def count(where):
        return jnp.sum(jnp.where(where, 1, 0), axis=1, keepdims=True)

    take, put = lax.bitwise_and(cell, 7), lax.shift_right_logical(cell, 3)
    if transposed:
        take, put = put, take
    put = jnp.where(lane < live, put, n_out)
    key = put * n + lane
    rank = count(key < column(key))
    hot = rank == lane
    again = count((put == column(put)) & (lane < line))
    last = jnp.where(count(put == line) > 0, count(put <= line) - 1, n)
    out[base : base + 1, 0:n] = line_sum(hot, line)
    out[base + 1 : base + 2, 0:n] = line_sum(hot, column(take))
    out[base + 2 : base + 3, 0:n] = line_sum(hot, again)
    out[base + 3 : base + 4, 0:n] = line_sum(lane == line, last)


class Ring:
    def __init__(self, ring, pair, slot, device):
        self.ring, self.pair = ring, pair
        self.slot_of, self.device_of = slot, device

    def at(self, dr, dp):
        return lax.rem(self.ring + dr, 4), (1 - self.pair) if dp else self.pair

    def slot(self, dr, dp, **kw):
        return self.slot_of(*self.at(dr, dp), **kw)

    def device(self, dr, dp):
        return self.device_of(*self.at(dr, dp))


class Net:
    def __init__(self, send_sems, recv_sems):
        self.send_sems, self.recv_sems = send_sems, recv_sems
        self.names, self.sends = {}, {}
        self.open = {}

    def send(self, src, dst, device, group, name):
        i = self.names.setdefault(name, len(self.names))
        now = self.open.setdefault(group, [])
        j = self.sends.setdefault((group, len(now)), len(self.sends))
        copy = pltpu.make_async_remote_copy(
            src_ref=src,
            dst_ref=dst,
            send_sem=self.send_sems.at[j],
            recv_sem=self.recv_sems.at[i],
            device_id=device,
            device_id_type=MESH,
        )
        copy.start()
        now.append(copy)
        return copy

    def arrived(self, ref, device, name):
        pltpu.make_async_remote_copy(
            src_ref=ref,
            dst_ref=ref,
            send_sem=self.send_sems.at[0],
            recv_sem=self.recv_sems.at[self.names[name]],
            device_id=device,
            device_id_type=MESH,
        ).wait_recv()

    def drain(self, group):
        for copy in self.open.pop(group, []):
            copy.wait_send()


def gather(net, geo, x, key, group, direct, partner=None):
    half = x.shape[1] // 2
    low, high = pl.ds(0, half), pl.ds(half, half)
    right, left, pair, far = geo.device(1, 0), geo.device(3, 0), geo.device(0, 1), geo.device(2, 0)
    net.drain(group)

    def send(ref, device, name):
        return net.send(ref, ref, device, group, (key, name))

    def share(dr, dp):
        if partner is not None:
            send(x.at[geo.slot(dr, dp)], partner, "share")

    mine, his = x.at[geo.slot(0, 0)], x.at[geo.slot(0, 1)]
    across = send(mine, pair, "across")
    own_r, own_l = send(mine, right, "own_r"), send(mine, left, "own_l")
    share(0, 0)
    yield
    own_r.wait_recv()
    far_a = send(x.at[geo.slot(3, 0), low], right, "far_a")
    own_l.wait_recv()
    far_b = send(x.at[geo.slot(1, 0), high], left, "far_b")
    share(3, 0)
    share(1, 0)
    yield
    across.wait_recv()
    other = [send(his, right, "other_r"), send(his, left, "other_l")]
    if direct:
        other.append(send(his, far, "other_f"))
    share(0, 1)
    yield
    far_a.wait_recv()
    far_b.wait_recv()
    if not direct:
        other.append(send(x.at[geo.slot(2, 0)], pair, "other_f"))
    share(2, 0)
    yield
    for c, dr in zip(other, (3, 1, 2)):
        c.wait_recv()
        share(dr, 1)
    yield
    if partner is not None:
        net.arrived(x.at[pl.ds(0, 8)], partner, (key, "share"))
    yield


ORDER = ((2, 1), (1, 1), (3, 1), (1, 0), (3, 0), (2, 0), (0, 1), (0, 0))
GROUPS = ((0, 1), (1, 4), (5, 1), (6, 2))


def place(dr, dp):
    return ORDER.index((dr, dp))


def scatter(net, geo, pick, s, buf, key, group, done, direct, partner=None, t=None, rc=None):
    ra, rp, rq, rd, total = buf
    half = s.shape[1] // 2
    low, high = pl.ds(0, half), pl.ds(half, half)
    right, left, pair, far = geo.device(1, 0), geo.device(3, 0), geo.device(0, 1), geo.device(2, 0)
    net.drain(group)

    def send(src, dst, device, name):
        return net.send(src, dst, device, group, (key, name))

    cores = []
    if partner is not None:
        for g, (begin, count) in enumerate(GROUPS):
            for i in range(begin, begin + count):
                t[i] = pick(geo.slot(*ORDER[i], other=True))
            there = pl.ds(begin, count)
            cores.append(send(t.at[there], rc.at[there], partner, ("core", g)))

    def bring(g):
        for i in range(GROUPS[g][0], sum(GROUPS[g])):
            s[i] = pick(geo.slot(*ORDER[i]))

    def add(g):
        if partner is not None:
            cores[g].wait_recv()
            for i in range(GROUPS[g][0], sum(GROUPS[g])):
                s[i] = (s[i].astype(F32) + rc[i].astype(F32)).astype(BF)

    def send_other():
        if direct:
            send(s.at[place(2, 1)], rq.at[2], far, "q")
        else:
            send(s.at[place(2, 1)], rq.at[2], pair, "far")

    def send_near():
        send(s.at[place(1, 1)], rq.at[0], right, "q")
        send(s.at[place(3, 1)], rq.at[1], left, "q")
        send(s.at[place(1, 0), high], rp.at[0, 1], right, "p")
        send(s.at[place(3, 0), low], rp.at[1, 0], left, "p")

    def send_far():
        i = place(2, 0)
        if not direct:
            net.arrived(rq.at[2], pair, (key, "far"))
            s[i] = (s[i].astype(F32) + rq[2].astype(F32)).astype(BF)
        return send(s.at[i, low], ra.at[0], right, "a"), send(s.at[i, high], ra.at[1], left, "b")

    if partner is None:
        bring(0)
        send_other()
        bring(1)
        send_near()
        bring(2)
        bring(3)
        yield
        yield
        first = send_far()
    else:
        for g in range(4):
            bring(g)
        yield
        add(0)
        send_other()
        add(1)
        send_near()
        yield
        add(2)
        first = send_far()
        add(3)
    yield
    i = place(0, 1)
    if direct:
        net.arrived(rq, pair, (key, "q"))
        s[i] = (s[i].astype(F32) + rq[0].astype(F32) + rq[1].astype(F32) + rq[2].astype(F32)).astype(BF)
    else:
        net.arrived(rq.at[pl.ds(0, 2)], pair, (key, "q"))
        s[i] = (s[i].astype(F32) + rq[0].astype(F32) + rq[1].astype(F32)).astype(BF)
    last = send(s.at[i], rd, pair, "last")
    yield
    to_r, to_l = place(1, 0), place(3, 0)
    first[0].wait_recv()
    s[to_r, low] = (s[to_r, low].astype(F32) + ra[0].astype(F32)).astype(BF)
    send(s.at[to_r, low], rp.at[0, 0], right, "p")
    first[1].wait_recv()
    s[to_l, high] = (s[to_l, high].astype(F32) + ra[1].astype(F32)).astype(BF)
    send(s.at[to_l, high], rp.at[1, 1], left, "p")
    yield
    net.arrived(rp, pair, (key, "p"))
    for h, rows in enumerate((low, high)):
        total[rows] = s[place(0, 0), rows].astype(F32) + rp[0, h].astype(F32) + rp[1, h].astype(F32)
    yield
    last.wait_recv()
    done(total[...] + rd[...].astype(F32))
    yield


def all_reduce(net, g, bufs, where, out, key):
    x, y, z, core, dev_x, dev_yz, partner = where
    b1, r1, h1, b2, r2, h2, b3, r3, gb = bufs
    n, m, w = h1.shape[0], h2.shape[0], b3.shape[2]
    plane = [(dy, dz) for dy in range(4) for dz in range(4) if (dy, dz) != (0, 0)]
    here = y * 4 + z

    def there(dy, dz):
        return lax.rem(y + dy, 4) * 4 + lax.rem(z + dz, 4)

    mine = pl.ds(pl.multiple_of(core * n, n), n)
    his = pl.ds(pl.multiple_of((1 - core) * n, n), n)
    b1[...] = g[his, :].astype(BF)
    c = net.send(b1, r1, partner, "g", (key, 1))
    yield
    c.wait_recv()
    h1[...] = g[mine, :] + r1[...].astype(F32)
    for k in range(16):
        b2[k] = h1[k * m : (k + 1) * m, :].astype(BF)
    for k, d in enumerate(plane):
        net.send(b2.at[there(*d)], r2.at[k], dev_yz(*d), "g", (key, 2))
    yield
    net.arrived(r2, partner, (key, 2))
    total = h1[pl.ds(pl.multiple_of(here * m, m), m), :]
    for k in range(15):
        total = total + r2[k].astype(F32)
    h2[...] = total
    for k in range(4):
        b3[k] = h2[:, k * w : (k + 1) * w].astype(BF)
    for d in (1, 2, 3):
        net.send(b3.at[lax.rem(x + d, 4)], r3.at[d - 1], dev_x(d), "g", (key, 3))
    yield
    net.arrived(r3, partner, (key, 3))
    piece = h2[:, pl.ds(pl.multiple_of(x * w, w), w)]
    piece = piece + r3[0].astype(F32) + r3[1].astype(F32) + r3[2].astype(F32)
    gb[core, here, x] = piece.astype(BF)
    ref = gb.at[core, here, x]
    for d in (1, 2, 3):
        net.send(ref, ref, dev_x(d), "g", (key, 4))
    yield
    net.arrived(gb.at[0, 0, pl.ds(0, 3)], partner, (key, 4))
    ref_p = gb.at[core, here]
    for d in plane:
        net.send(ref_p, ref_p, dev_yz(*d), "g", (key, 5))
    yield
    net.arrived(gb.at[0, pl.ds(0, 15)], partner, (key, 5))
    ref_c = gb.at[core]
    c = net.send(ref_c, ref_c, partner, "g", (key, 6))
    yield
    c.wait_recv()

    def write(i, carry):
        for k in range(4):
            begin = pl.multiple_of(i * m, m)
            out[pl.ds(begin, m), k * w : (k + 1) * w] = gb[i // 16, lax.rem(i, 16), k]
        return carry

    lax.fori_loop(0, 32, write, 0, unroll=4)
    yield


def slope(pre):
    sig = jax.nn.sigmoid(pre)
    return sig * (1.0 + pre * (1.0 - sig))


def dot_rows(a, b):
    return lax.dot_general(a, b, (((0,), (0,)), ((), ())), preferred_element_type=F32)


def dot_cols(a, b):
    return lax.dot_general(a, b, (((1,), (1,)), ((), ())), preferred_element_type=F32)


def dot(a, b):
    return jnp.dot(a, b, preferred_element_type=F32)


WIDTHS = (128, 256, 128)
PROGRAM = (
    "O0", "O1", "F", "H0", "Q0", "O2", "S", "H1", "Q1", "K0", "H2", "K1", "Q2", "E0", "G0", "S", "T0", "P0",
    "K2", "U0", "E1", "G1", "S", "T1", "P1", "V0", "U1", "E2", "G2", "T2", "P2", "V1", "U2", "C0", "S", "B0",
    "V2", "C1", "B1", "S", "D0", "C2", "B2", "Z0", "D1", "Z1", "S", "D2", "Z2",
)
GATHER_DIRECT = (False, False, False)
SCATTER_DIRECT = (False, False, False)
SETS = {"f1": 0, "f2": 1, "b2": 0, "b1": 1}
UNROLL = 8


def kernel(names, cells, live, features, values_hbm, w_first_hbm, w_second_hbm, cotangent_hbm,
           out_act, grad_input, grad_first, grad_second, *scratch):
    m = dict(zip(names, scratch))
    row, col = lax.axis_index("row"), lax.axis_index("col")
    y, zl = row // 2, lax.rem(row, 2)
    zh, x, core = col // 8, lax.rem(col // 2, 4), lax.rem(col, 2)
    z = zh * 2 + zl

    def col_slot(r, p, other=False):
        return p * 8 + r * 2 + ((1 - core) if other else core)

    rows = Ring(y, zl, lambda r, p: r * 2 + p, lambda r, p: (r * 2 + p, col))
    cols = Ring(x, zh, col_slot, lambda r, p: (row, col_slot(r, p)))
    partner = (row, col_slot(x, zh, other=True))

    def dev_x(d):
        return cols.device(d, 0)

    def dev_yz(dy, dz):
        there = lax.rem(z + dz, 4)
        return (lax.rem(y + dy, 4) * 2 + lax.rem(there, 2), col_slot(x, there // 2))

    w_first, w_second, cotangent, plan = m["w1"], m["w2"], m["cot"], m["plan"]
    loads = [
        pltpu.make_async_copy(src, dst, m["load_sems"].at[i])
        for i, (src, dst) in enumerate(
            ((values_hbm, m["a"]), (w_first_hbm, w_first), (w_second_hbm, w_second), (cotangent_hbm, cotangent))
        )
    ]

    barrier = pltpu.get_barrier_semaphore()
    peers = [dev_x(d) for d in (1, 2, 3)] + [partner]
    peers += [dev_yz(dy, dz) for dy in range(4) for dz in range(4) if (dy, dz) != (0, 0)]
    for peer in peers:
        pl.semaphore_signal(barrier, inc=1, device_id=peer, device_id_type=MESH)
    for load in loads:
        load.start()

    net = Net(m["send_sems"], m["recv_sems"])
    nl, width = features.shape
    chunks, begin = [], 0
    for w in WIDTHS:
        chunks.append(slice(begin, begin + w))
        begin += w
    n_chunks = len(chunks)
    n_slots = m["a"].shape[0]
    for w in sorted(set(WIDTHS)):
        prod = m["prod", w]
        prod[n_slots] = jnp.zeros(prod.shape[1:], BF)

    def tile(a, xc, base, w):
        prod, acc = m["prod", w], m["acc", w]
        acc[...] = jnp.zeros_like(acc)

        def step(i, carry):
            p = dot(a[plan[base, i]], xc[plan[base + 1, i]])
            v = jnp.where(plan[base + 2, i] > 0, acc[...], 0.0) + p
            acc[...] = v
            prod[i] = v.astype(BF)
            return carry

        lax.fori_loop(0, n_slots, step, 0, unroll=UNROLL)

    reduces = []

    def side(steps=1):
        for _ in range(steps):
            for g in reduces:
                next(g, None)

    def aggregate(name, back, own, filler, done):
        a = m["at"] if back else m["a"]
        base = 4 if back else 0
        geo_in, geo_out = (cols, rows) if back else (rows, cols)
        k = SETS[name]
        ag, rs = [], []
        for c, w in enumerate(WIDTHS):
            def pick(slot, prod=m["prod", w]):
                return prod[plan[base + 3, slot]]

            ag.append(
                gather(net, geo_in, m["x", name, c], ("x", k, c), ("x", c), GATHER_DIRECT[c], partner if back else None)
            )
            more = {} if back else {"partner": partner, "t": m["t", c], "rc": m["rc", name, c]}
            bufs = tuple(m[q, name, c] for q in ("ra", "rp", "rq", "rd")) + (m["total", c],)
            rs.append(
                scatter(
                    net, geo_out, pick, m["s", c], bufs, ("s", k, c), ("s", c),
                    functools.partial(done, c), SCATTER_DIRECT[c], **more,
                )
            )
        for word in PROGRAM:
            c = int(word[1:] or 0)
            if word[0] == "O":
                m["x", name, c][geo_in.slot(0, 0)] = own(c).astype(BF)
                if name == "f1" and c == 0:
                    pl.semaphore_wait(barrier, len(peers))
                next(ag[c])
            elif word[0] in "HQKEG":
                next(ag[c])
            elif word[0] == "T":
                tile(a, m["x", name, c], base, WIDTHS[c])
            elif word[0] == "S":
                side()
            elif word[0] == "F":
                filler()
            else:
                next(rs[c])

    agg, pre_first, pre_second, d_second, d_first = (m[q] for q in ("agg", "pre1", "pre2", "d2", "d1"))

    def layer(k, pre, w):
        def done(c, value):
            agg[k, :, chunks[c]] = value.astype(BF)
            part = dot(agg[k, :, chunks[c]], w[chunks[c], :])
            pre[...] = part if c == 0 else pre[...] + part

        return done

    def wait_loads():
        slot_plan(cells, live[0, 0], m["lines"], 0, 16, False)
        slot_plan(cells, live[0, 0], m["lines"], 4, 8, True)
        move = pltpu.make_async_copy(m["lines"], plan, m["load_sems"].at[4])
        move.start()
        move.wait()
        for load in loads:
            load.wait()

    aggregate("f1", False, lambda c: features[:, chunks[c]], wait_loads, layer(0, pre_first, w_first))

    def turn():
        def one(i, carry):
            m["at"][i] = m["a"][i].T
            return carry

        lax.fori_loop(0, n_slots, one, 0)

    aggregate(
        "f2", False, lambda c: jax.nn.silu(pre_first[:, chunks[c]]), turn, layer(1, pre_second, w_second)
    )
    for c in chunks:
        u = pre_second[:, c]
        d_second[:, c] = (cotangent[:, c].astype(F32) * slope(u)).astype(BF)

    where = (x, y, z, core, dev_x, dev_yz, partner)

    def weight_grad(k, d, out, name):
        g = m["grad", name]
        half = width // 2
        for c in (slice(0, half), slice(half, width)):
            g[c, :] = dot_rows(agg[k, :, c], d[...])
        reduces.append(all_reduce(net, g, [m[q, name] for q in AR_KEYS], where, out, ("g", name)))
        side()

    def hidden_back(c, value):
        d_first[:, chunks[c]] = (value * slope(pre_first[:, chunks[c]])).astype(BF)

    def second_grad():
        out_act[...] = jax.nn.silu(pre_second[...]).astype(BF)
        weight_grad(1, d_second, grad_second, "g2")

    aggregate("b2", True, lambda c: dot_cols(d_second[...], w_second[chunks[c], :]), second_grad, hidden_back)

    def input_back(c, value):
        grad_input[:, chunks[c]] = value.astype(BF)

    aggregate(
        "b1", True, lambda c: dot_cols(d_first[...], w_first[chunks[c], :]),
        lambda: weight_grad(0, d_first, grad_first, "g1"), input_back,
    )
    side(12)
    for group in list(net.open):
        net.drain(group)


AR_KEYS = ("b1", "r1", "h1", "b2", "r2", "h2", "b3", "r3", "gb")


def scratch_of(nl, width, side, slots):
    s = {}

    def add(key, shape, kind=BF):
        s[key] = pltpu.VMEM(shape, kind)

    add("a", (slots, side, side))
    add("at", (slots, side, side))
    add("w1", (width, width))
    add("w2", (width, width))
    add("cot", (nl, width))
    for w in sorted(set(WIDTHS)):
        add(("prod", w), (slots + 1, side, w))
        add(("acc", w), (side, w), F32)
    for c, w in enumerate(WIDTHS):
        add(("s", c), (8, nl, w))
        add(("t", c), (8, nl, w))
        add(("total", c), (nl, w), F32)
        for name, blocks in (("f1", 8), ("f2", 8), ("b2", 16), ("b1", 16)):
            add(("x", name, c), (blocks, nl, w))
            add(("ra", name, c), (2, nl // 2, w))
            add(("rp", name, c), (2, 2, nl // 2, w))
            add(("rq", name, c), (3, nl, w))
            add(("rd", name, c), (nl, w))
            if blocks == 8:
                add(("rc", name, c), (8, nl, w))
    add("agg", (2, nl, width))
    add("pre1", (nl, width), F32)
    add("pre2", (nl, width), F32)
    add("d2", (nl, width))
    add("d1", (nl, width))
    h = width
    for name in ("g2", "g1"):
        add(("grad", name), (width, width), F32)
        add(("b1", name), (h // 2, width))
        add(("r1", name), (h // 2, width))
        add(("h1", name), (h // 2, width), F32)
        add(("b2", name), (16, h // 32, width))
        add(("r2", name), (15, h // 32, width))
        add(("h2", name), (h // 32, width), F32)
        add(("b3", name), (4, h // 32, width // 4))
        add(("r3", name), (3, h // 32, width // 4))
        add(("gb", name), (2, 16, 4, h // 32, width // 4))
    s["lines"] = pltpu.VMEM((8, 128), jnp.int32)
    s["plan"] = pltpu.SMEM((8, 128), jnp.int32)
    s["load_sems"] = pltpu.SemaphoreType.DMA((5,))
    n = len(WIDTHS)
    s["send_sems"] = pltpu.SemaphoreType.DMA((30 * n + 76,))
    s["recv_sems"] = pltpu.SemaphoreType.DMA((38 * n + 14,))
    return s


def tail(out_act, grad_input, grad_first, grad_second, out_act_t, grad_input_t, grad_first_t, grad_second_t):
    out_act_t[...] = out_act[...]
    grad_input_t[...] = grad_input[...]
    grad_first_t[...] = grad_first[...].astype(F32)
    grad_second_t[...] = grad_second[...].astype(F32)


def local(features, adj_values, block_cells, block_counts, w_first, w_second, cotangent):
    values, cells = adj_values[0, 0], block_cells[0]
    nl, width = features.shape
    slots, side, _ = values.shape
    scratch = scratch_of(nl, width, side, slots)
    vmem = pl.BlockSpec(memory_space=pltpu.VMEM)
    hbm = pl.BlockSpec(memory_space=pl.ANY)

    def shapes(kind):
        node, weight = jax.ShapeDtypeStruct((nl, width), BF), jax.ShapeDtypeStruct((width, width), kind)
        return (node, node, weight, weight)

    outs = pl.pallas_call(
        functools.partial(kernel, tuple(scratch)),
        out_shape=shapes(BF),
        in_specs=[vmem, pl.BlockSpec(memory_space=pltpu.SMEM), vmem, hbm, hbm, hbm, hbm],
        out_specs=(vmem, vmem, vmem, vmem),
        scratch_shapes=list(scratch.values()),
        compiler_params=pltpu.CompilerParams(
            collective_id=0, has_side_effects=True, vmem_limit_bytes=63 * 1024 * 1024 - 512 * 1024
        ),
    )(cells, block_counts, features, values, w_first, w_second, cotangent)
    return pl.pallas_call(
        tail,
        out_shape=shapes(F32),
        in_specs=[vmem] * 4,
        out_specs=(vmem,) * 4,
        compiler_params=pltpu.CompilerParams(vmem_limit_bytes=16 * 1024 * 1024),
    )(*outs)


def solution(mesh):
    return jax.shard_map(
        local,
        mesh=mesh,
        in_specs=(
            P(("row", "col"), None),
            P("row", "col", None, None, None),
            P("row", "col", None),
            P("row", "col"),
            P(),
            P(),
            P(("row", "col"), None),
        ),
        out_specs=(P(("row", "col"), None), P(("row", "col"), None), P(), P()),
        check_vma=False,
    )
```

```python
import functools

import jax
import jax.numpy as jnp
from jax import lax
from jax.experimental import pallas as pl
from jax.experimental.pallas import tpu as pltpu
from jax.sharding import PartitionSpec as P

MESH = pl.DeviceIdType.MESH
BF = jnp.bfloat16
F32 = jnp.float32


def slot_plan(cells, live, out, base, n_out, transposed):
    n = cells.shape[1]
    lane = lax.broadcasted_iota(jnp.int32, (n, n), 1)
    line = lax.broadcasted_iota(jnp.int32, (n, n), 0)
    cell = jnp.broadcast_to(cells[...], (n, n))

    def column(a):
        return jnp.sum(jnp.where(lane == line, a, 0), axis=1, keepdims=True)

    def line_sum(where, a):
        return jnp.sum(jnp.where(where, a, 0), axis=0, keepdims=True)

    def count(where):
        return jnp.sum(jnp.where(where, 1, 0), axis=1, keepdims=True)

    take, put = lax.bitwise_and(cell, 7), lax.shift_right_logical(cell, 3)
    if transposed:
        take, put = put, take
    put = jnp.where(lane < live, put, n_out)
    key = put * n + lane
    rank = count(key < column(key))
    hot = rank == lane
    again = count((put == column(put)) & (lane < line))
    last = jnp.where(count(put == line) > 0, count(put <= line) - 1, n)
    out[base : base + 1, 0:n] = line_sum(hot, line)
    out[base + 1 : base + 2, 0:n] = line_sum(hot, column(take))
    out[base + 2 : base + 3, 0:n] = line_sum(hot, again)
    out[base + 3 : base + 4, 0:n] = line_sum(lane == line, last)


class Ring:
    def __init__(self, ring, pair, slot, device):
        self.ring, self.pair = ring, pair
        self.slot_of, self.device_of = slot, device

    def at(self, dr, dp):
        return lax.rem(self.ring + dr, 4), (1 - self.pair) if dp else self.pair

    def slot(self, dr, dp, **kw):
        return self.slot_of(*self.at(dr, dp), **kw)

    def device(self, dr, dp):
        return self.device_of(*self.at(dr, dp))


class Net:
    def __init__(self, send_sems, recv_sems):
        self.send_sems, self.recv_sems = send_sems, recv_sems
        self.names, self.sends = {}, {}
        self.open = {}

    def send(self, src, dst, device, group, name):
        i = self.names.setdefault(name, len(self.names))
        now = self.open.setdefault(group, [])
        j = self.sends.setdefault((group, len(now)), len(self.sends))
        copy = pltpu.make_async_remote_copy(
            src_ref=src,
            dst_ref=dst,
            send_sem=self.send_sems.at[j],
            recv_sem=self.recv_sems.at[i],
            device_id=device,
            device_id_type=MESH,
        )
        copy.start()
        now.append(copy)
        return copy

    def arrived(self, ref, device, name):
        pltpu.make_async_remote_copy(
            src_ref=ref,
            dst_ref=ref,
            send_sem=self.send_sems.at[0],
            recv_sem=self.recv_sems.at[self.names[name]],
            device_id=device,
            device_id_type=MESH,
        ).wait_recv()

    def drain(self, group):
        for copy in self.open.pop(group, []):
            copy.wait_send()


def gather(net, geo, x, key, group, direct, partner=None):
    half = x.shape[1] // 2
    low, high = pl.ds(0, half), pl.ds(half, half)
    right, left, pair, far = geo.device(1, 0), geo.device(3, 0), geo.device(0, 1), geo.device(2, 0)
    net.drain(group)

    def send(ref, device, name):
        return net.send(ref, ref, device, group, (key, name))

    def share(dr, dp):
        if partner is not None:
            send(x.at[geo.slot(dr, dp)], partner, "share")

    mine, his = x.at[geo.slot(0, 0)], x.at[geo.slot(0, 1)]
    across = send(mine, pair, "across")
    own_r, own_l = send(mine, right, "own_r"), send(mine, left, "own_l")
    share(0, 0)
    yield
    own_r.wait_recv()
    far_a = send(x.at[geo.slot(3, 0), low], right, "far_a")
    own_l.wait_recv()
    far_b = send(x.at[geo.slot(1, 0), high], left, "far_b")
    share(3, 0)
    share(1, 0)
    yield
    across.wait_recv()
    other = [send(his, right, "other_r"), send(his, left, "other_l")]
    if direct:
        other.append(send(his, far, "other_f"))
    share(0, 1)
    yield
    far_a.wait_recv()
    far_b.wait_recv()
    if not direct:
        other.append(send(x.at[geo.slot(2, 0)], pair, "other_f"))
    share(2, 0)
    yield
    for c, dr in zip(other, (3, 1, 2)):
        c.wait_recv()
        share(dr, 1)
    yield
    if partner is not None:
        net.arrived(x.at[pl.ds(0, 8)], partner, (key, "share"))
    yield


ORDER = ((2, 1), (1, 1), (3, 1), (1, 0), (3, 0), (2, 0), (0, 1), (0, 0))
GROUPS = ((0, 1), (1, 4), (5, 1), (6, 2))


def place(dr, dp):
    return ORDER.index((dr, dp))


def scatter(net, geo, pick, s, buf, key, group, done, direct, partner=None, t=None, rc=None):
    ra, rp, rq, rd, total = buf
    half = s.shape[1] // 2
    low, high = pl.ds(0, half), pl.ds(half, half)
    right, left, pair, far = geo.device(1, 0), geo.device(3, 0), geo.device(0, 1), geo.device(2, 0)
    net.drain(group)

    def send(src, dst, device, name):
        return net.send(src, dst, device, group, (key, name))

    cores = []
    if partner is not None:
        for g, (begin, count) in enumerate(GROUPS):
            for i in range(begin, begin + count):
                t[i] = pick(geo.slot(*ORDER[i], other=True))
            there = pl.ds(begin, count)
            cores.append(send(t.at[there], rc.at[there], partner, ("core", g)))

    def bring(g):
        for i in range(GROUPS[g][0], sum(GROUPS[g])):
            s[i] = pick(geo.slot(*ORDER[i]))

    def add(g):
        if partner is not None:
            cores[g].wait_recv()
            for i in range(GROUPS[g][0], sum(GROUPS[g])):
                s[i] = (s[i].astype(F32) + rc[i].astype(F32)).astype(BF)

    def send_other():
        if direct:
            send(s.at[place(2, 1)], rq.at[2], far, "q")
        else:
            send(s.at[place(2, 1)], rq.at[2], pair, "far")

    def send_near():
        send(s.at[place(1, 1)], rq.at[0], right, "q")
        send(s.at[place(3, 1)], rq.at[1], left, "q")
        send(s.at[place(1, 0), high], rp.at[0, 1], right, "p")
        send(s.at[place(3, 0), low], rp.at[1, 0], left, "p")

    def send_far():
        i = place(2, 0)
        if not direct:
            net.arrived(rq.at[2], pair, (key, "far"))
            s[i] = (s[i].astype(F32) + rq[2].astype(F32)).astype(BF)
        return send(s.at[i, low], ra.at[0], right, "a"), send(s.at[i, high], ra.at[1], left, "b")

    if partner is None:
        bring(0)
        send_other()
        bring(1)
        send_near()
        bring(2)
        bring(3)
        yield
        yield
        first = send_far()
    else:
        for g in range(4):
            bring(g)
        yield
        add(0)
        send_other()
        add(1)
        send_near()
        yield
        add(2)
        first = send_far()
        add(3)
    yield
    i = place(0, 1)
    if direct:
        net.arrived(rq, pair, (key, "q"))
        s[i] = (s[i].astype(F32) + rq[0].astype(F32) + rq[1].astype(F32) + rq[2].astype(F32)).astype(BF)
    else:
        net.arrived(rq.at[pl.ds(0, 2)], pair, (key, "q"))
        s[i] = (s[i].astype(F32) + rq[0].astype(F32) + rq[1].astype(F32)).astype(BF)
    last = send(s.at[i], rd, pair, "last")
    yield
    to_r, to_l = place(1, 0), place(3, 0)
    first[0].wait_recv()
    s[to_r, low] = (s[to_r, low].astype(F32) + ra[0].astype(F32)).astype(BF)
    send(s.at[to_r, low], rp.at[0, 0], right, "p")
    first[1].wait_recv()
    s[to_l, high] = (s[to_l, high].astype(F32) + ra[1].astype(F32)).astype(BF)
    send(s.at[to_l, high], rp.at[1, 1], left, "p")
    yield
    net.arrived(rp, pair, (key, "p"))
    for h, rows in enumerate((low, high)):
        total[rows] = s[place(0, 0), rows].astype(F32) + rp[0, h].astype(F32) + rp[1, h].astype(F32)
    yield
    last.wait_recv()
    done(total[...] + rd[...].astype(F32))
    yield


def all_reduce(net, g, bufs, where, out, key):
    x, y, z, core, dev_x, dev_yz, partner = where
    b1, r1, h1, b2, r2, h2, b3, r3, gb = bufs
    n, m, w = h1.shape[0], h2.shape[0], b3.shape[2]
    plane = [(dy, dz) for dy in range(4) for dz in range(4) if (dy, dz) != (0, 0)]
    here = y * 4 + z

    def there(dy, dz):
        return lax.rem(y + dy, 4) * 4 + lax.rem(z + dz, 4)

    mine = pl.ds(pl.multiple_of(core * n, n), n)
    his = pl.ds(pl.multiple_of((1 - core) * n, n), n)
    b1[...] = g[his, :].astype(BF)
    c = net.send(b1, r1, partner, "g", (key, 1))
    yield
    c.wait_recv()
    h1[...] = g[mine, :] + r1[...].astype(F32)
    for k in range(16):
        b2[k] = h1[k * m : (k + 1) * m, :].astype(BF)
    for k, d in enumerate(plane):
        net.send(b2.at[there(*d)], r2.at[k], dev_yz(*d), "g", (key, 2))
    yield
    net.arrived(r2, partner, (key, 2))
    total = h1[pl.ds(pl.multiple_of(here * m, m), m), :]
    for k in range(15):
        total = total + r2[k].astype(F32)
    h2[...] = total
    for k in range(4):
        b3[k] = h2[:, k * w : (k + 1) * w].astype(BF)
    for d in (1, 2, 3):
        net.send(b3.at[lax.rem(x + d, 4)], r3.at[d - 1], dev_x(d), "g", (key, 3))
    yield
    net.arrived(r3, partner, (key, 3))
    piece = h2[:, pl.ds(pl.multiple_of(x * w, w), w)]
    piece = piece + r3[0].astype(F32) + r3[1].astype(F32) + r3[2].astype(F32)
    gb[core, here, x] = piece.astype(BF)
    ref = gb.at[core, here, x]
    for d in (1, 2, 3):
        net.send(ref, ref, dev_x(d), "g", (key, 4))
    yield
    net.arrived(gb.at[0, 0, pl.ds(0, 3)], partner, (key, 4))
    ref_p = gb.at[core, here]
    for d in plane:
        net.send(ref_p, ref_p, dev_yz(*d), "g", (key, 5))
    yield
    net.arrived(gb.at[0, pl.ds(0, 15)], partner, (key, 5))
    ref_c = gb.at[core]
    c = net.send(ref_c, ref_c, partner, "g", (key, 6))
    yield
    c.wait_recv()

    def write(i, carry):
        for k in range(4):
            begin = pl.multiple_of(i * m, m)
            out[pl.ds(begin, m), k * w : (k + 1) * w] = gb[i // 16, lax.rem(i, 16), k]
        return carry

    lax.fori_loop(0, 32, write, 0, unroll=4)
    yield


def slope(pre):
    sig = jax.nn.sigmoid(pre)
    return sig * (1.0 + pre * (1.0 - sig))


def dot_rows(a, b):
    return lax.dot_general(a, b, (((0,), (0,)), ((), ())), preferred_element_type=F32)


def dot_cols(a, b):
    return lax.dot_general(a, b, (((1,), (1,)), ((), ())), preferred_element_type=F32)


def dot(a, b):
    return jnp.dot(a, b, preferred_element_type=F32)


WIDTHS = (128, 256, 128)
PROGRAM = (
    "O0", "O1", "F", "H0", "Q0", "O2", "S", "H1", "Q1", "K0", "H2", "K1", "Q2", "E0", "G0", "S", "T0", "P0",
    "K2", "U0", "E1", "G1", "S", "T1", "P1", "V0", "U1", "E2", "G2", "T2", "P2", "V1", "U2", "C0", "S", "B0",
    "V2", "C1", "B1", "S", "D0", "C2", "B2", "Z0", "D1", "Z1", "S", "D2", "Z2",
)
GATHER_DIRECT = (False, False, False)
SCATTER_DIRECT = (False, False, False)
SETS = {"f1": 0, "f2": 1, "b2": 0, "b1": 1}
UNROLL = 8


def kernel(names, cells, live, features, values_hbm, w_first_hbm, w_second_hbm, cotangent_hbm,
           out_act, grad_input, grad_first, grad_second, *scratch):
    m = dict(zip(names, scratch))
    row, col = lax.axis_index("row"), lax.axis_index("col")
    y, zl = row // 2, lax.rem(row, 2)
    zh, x, core = col // 8, lax.rem(col // 2, 4), lax.rem(col, 2)
    z = zh * 2 + zl

    def col_slot(r, p, other=False):
        return p * 8 + r * 2 + ((1 - core) if other else core)

    rows = Ring(y, zl, lambda r, p: r * 2 + p, lambda r, p: (r * 2 + p, col))
    cols = Ring(x, zh, col_slot, lambda r, p: (row, col_slot(r, p)))
    partner = (row, col_slot(x, zh, other=True))

    def dev_x(d):
        return cols.device(d, 0)

    def dev_yz(dy, dz):
        there = lax.rem(z + dz, 4)
        return (lax.rem(y + dy, 4) * 2 + lax.rem(there, 2), col_slot(x, there // 2))

    w_first, w_second, cotangent, plan = m["w1"], m["w2"], m["cot"], m["plan"]
    loads = [
        pltpu.make_async_copy(src, dst, m["load_sems"].at[i])
        for i, (src, dst) in enumerate(
            ((values_hbm, m["a"]), (w_first_hbm, w_first), (w_second_hbm, w_second), (cotangent_hbm, cotangent))
        )
    ]

    barrier = pltpu.get_barrier_semaphore()
    peers = [dev_x(d) for d in (1, 2, 3)] + [partner]
    peers += [dev_yz(dy, dz) for dy in range(4) for dz in range(4) if (dy, dz) != (0, 0)]
    for peer in peers:
        pl.semaphore_signal(barrier, inc=1, device_id=peer, device_id_type=MESH)
    for load in loads:
        load.start()

    net = Net(m["send_sems"], m["recv_sems"])
    nl, width = features.shape
    chunks, begin = [], 0
    for w in WIDTHS:
        chunks.append(slice(begin, begin + w))
        begin += w
    n_chunks = len(chunks)
    n_slots = m["a"].shape[0]
    for w in sorted(set(WIDTHS)):
        prod = m["prod", w]
        prod[n_slots] = jnp.zeros(prod.shape[1:], BF)

    def tile(a, xc, base, w):
        prod, acc = m["prod", w], m["acc", w]
        acc[...] = jnp.zeros_like(acc)

        def step(i, carry):
            p = dot(a[plan[base, i]], xc[plan[base + 1, i]])
            v = jnp.where(plan[base + 2, i] > 0, acc[...], 0.0) + p
            acc[...] = v
            prod[i] = v.astype(BF)
            return carry

        lax.fori_loop(0, n_slots, step, 0, unroll=UNROLL)

    reduces = []

    def side(steps=1):
        for _ in range(steps):
            for g in reduces:
                next(g, None)

    def aggregate(name, back, own, filler, done):
        a = m["at"] if back else m["a"]
        base = 4 if back else 0
        geo_in, geo_out = (cols, rows) if back else (rows, cols)
        k = SETS[name]
        ag, rs = [], []
        for c, w in enumerate(WIDTHS):
            def pick(slot, prod=m["prod", w]):
                return prod[plan[base + 3, slot]]

            ag.append(
                gather(net, geo_in, m["x", name, c], ("x", k, c), ("x", c), GATHER_DIRECT[c], partner if back else None)
            )
            more = {} if back else {"partner": partner, "t": m["t", c], "rc": m["rc", name, c]}
            bufs = tuple(m[q, name, c] for q in ("ra", "rp", "rq", "rd")) + (m["total", c],)
            rs.append(
                scatter(
                    net, geo_out, pick, m["s", c], bufs, ("s", k, c), ("s", c),
                    functools.partial(done, c), SCATTER_DIRECT[c], **more,
                )
            )
        for word in PROGRAM:
            c = int(word[1:] or 0)
            if word[0] == "O":
                m["x", name, c][geo_in.slot(0, 0)] = own(c).astype(BF)
                if name == "f1" and c == 0:
                    pl.semaphore_wait(barrier, len(peers))
                next(ag[c])
            elif word[0] in "HQKEG":
                next(ag[c])
            elif word[0] == "T":
                tile(a, m["x", name, c], base, WIDTHS[c])
            elif word[0] == "S":
                side()
            elif word[0] == "F":
                filler()
            else:
                next(rs[c])

    agg, pre_first, pre_second, d_second, d_first = (m[q] for q in ("agg", "pre1", "pre2", "d2", "d1"))

    def layer(k, pre, w):
        def done(c, value):
            agg[k, :, chunks[c]] = value.astype(BF)
            part = dot(agg[k, :, chunks[c]], w[chunks[c], :])
            pre[...] = part if c == 0 else pre[...] + part

        return done

    def wait_loads():
        slot_plan(cells, live[0, 0], m["lines"], 0, 16, False)
        slot_plan(cells, live[0, 0], m["lines"], 4, 8, True)
        move = pltpu.make_async_copy(m["lines"], plan, m["load_sems"].at[4])
        move.start()
        move.wait()
        for load in loads:
            load.wait()

    aggregate("f1", False, lambda c: features[:, chunks[c]], wait_loads, layer(0, pre_first, w_first))

    def turn():
        def one(i, carry):
            m["at"][i] = m["a"][i].T
            return carry

        lax.fori_loop(0, n_slots, one, 0)

    aggregate(
        "f2", False, lambda c: jax.nn.silu(pre_first[:, chunks[c]]), turn, layer(1, pre_second, w_second)
    )
    for c in chunks:
        u = pre_second[:, c]
        d_second[:, c] = (cotangent[:, c].astype(F32) * slope(u)).astype(BF)

    where = (x, y, z, core, dev_x, dev_yz, partner)

    def weight_grad(k, d, out, name):
        g = m["grad", name]
        half = width // 2
        for c in (slice(0, half), slice(half, width)):
            g[c, :] = dot_rows(agg[k, :, c], d[...])
        reduces.append(all_reduce(net, g, [m[q, name] for q in AR_KEYS], where, out, ("g", name)))
        side()

    def hidden_back(c, value):
        d_first[:, chunks[c]] = (value * slope(pre_first[:, chunks[c]])).astype(BF)

    def second_grad():
        out_act[...] = jax.nn.silu(pre_second[...]).astype(BF)
        weight_grad(1, d_second, grad_second, "g2")

    aggregate("b2", True, lambda c: dot_cols(d_second[...], w_second[chunks[c], :]), second_grad, hidden_back)

    def input_back(c, value):
        grad_input[:, chunks[c]] = value.astype(BF)

    aggregate(
        "b1", True, lambda c: dot_cols(d_first[...], w_first[chunks[c], :]),
        lambda: weight_grad(0, d_first, grad_first, "g1"), input_back,
    )
    side(12)
    for group in list(net.open):
        net.drain(group)


AR_KEYS = ("b1", "r1", "h1", "b2", "r2", "h2", "b3", "r3", "gb")


def scratch_of(nl, width, side, slots):
    s = {}

    def add(key, shape, kind=BF):
        s[key] = pltpu.VMEM(shape, kind)

    add("a", (slots, side, side))
    add("at", (slots, side, side))
    add("w1", (width, width))
    add("w2", (width, width))
    add("cot", (nl, width))
    for w in sorted(set(WIDTHS)):
        add(("prod", w), (slots + 1, side, w))
        add(("acc", w), (side, w), F32)
    for c, w in enumerate(WIDTHS):
        add(("s", c), (8, nl, w))
        add(("t", c), (8, nl, w))
        add(("total", c), (nl, w), F32)
        for name, blocks in (("f1", 8), ("f2", 8), ("b2", 16), ("b1", 16)):
            add(("x", name, c), (blocks, nl, w))
            add(("ra", name, c), (2, nl // 2, w))
            add(("rp", name, c), (2, 2, nl // 2, w))
            add(("rq", name, c), (3, nl, w))
            add(("rd", name, c), (nl, w))
            if blocks == 8:
                add(("rc", name, c), (8, nl, w))
    add("agg", (2, nl, width))
    add("pre1", (nl, width), F32)
    add("pre2", (nl, width), F32)
    add("d2", (nl, width))
    add("d1", (nl, width))
    h = width
    for name in ("g2", "g1"):
        add(("grad", name), (width, width), F32)
        add(("b1", name), (h // 2, width))
        add(("r1", name), (h // 2, width))
        add(("h1", name), (h // 2, width), F32)
        add(("b2", name), (16, h // 32, width))
        add(("r2", name), (15, h // 32, width))
        add(("h2", name), (h // 32, width), F32)
        add(("b3", name), (4, h // 32, width // 4))
        add(("r3", name), (3, h // 32, width // 4))
        add(("gb", name), (2, 16, 4, h // 32, width // 4))
    s["lines"] = pltpu.VMEM((8, 128), jnp.int32)
    s["plan"] = pltpu.SMEM((8, 128), jnp.int32)
    s["load_sems"] = pltpu.SemaphoreType.DMA((5,))
    n = len(WIDTHS)
    s["send_sems"] = pltpu.SemaphoreType.DMA((30 * n + 76,))
    s["recv_sems"] = pltpu.SemaphoreType.DMA((38 * n + 14,))
    return s


def tail(
    out_act, grad_input, grad_first, grad_second, out_act_t, grad_input_t, grad_first_t, grad_second_t, first, second, sems
):
    pairs = ((grad_first, first), (grad_second, second), (out_act, out_act_t), (grad_input, grad_input_t))
    copies = [pltpu.make_async_copy(src, dst, sems.at[i]) for i, (src, dst) in enumerate(pairs)]
    for copy in copies:
        copy.start()
    copies[0].wait()
    grad_first_t[...] = first[...].astype(F32)
    copies[1].wait()
    grad_second_t[...] = second[...].astype(F32)
    copies[2].wait()
    copies[3].wait()


def local(features, adj_values, block_cells, block_counts, w_first, w_second, cotangent):
    values, cells = adj_values[0, 0], block_cells[0]
    nl, width = features.shape
    slots, side, _ = values.shape
    scratch = scratch_of(nl, width, side, slots)
    vmem = pl.BlockSpec(memory_space=pltpu.VMEM)
    hbm = pl.BlockSpec(memory_space=pl.ANY)

    def shapes(kind):
        node, weight = jax.ShapeDtypeStruct((nl, width), BF), jax.ShapeDtypeStruct((width, width), kind)
        return (node, node, weight, weight)

    outs = pl.pallas_call(
        functools.partial(kernel, tuple(scratch)),
        out_shape=shapes(BF),
        in_specs=[vmem, pl.BlockSpec(memory_space=pltpu.SMEM), vmem, hbm, hbm, hbm, hbm],
        out_specs=(vmem, vmem, vmem, vmem),
        scratch_shapes=list(scratch.values()),
        compiler_params=pltpu.CompilerParams(
            collective_id=0, has_side_effects=True, vmem_limit_bytes=63 * 1024 * 1024 - 512 * 1024
        ),
    )(cells, block_counts, features, values, w_first, w_second, cotangent)
    return pl.pallas_call(
        tail,
        out_shape=shapes(F32),
        in_specs=[hbm] * 4,
        out_specs=(vmem,) * 4,
        scratch_shapes=[pltpu.VMEM((width, width), BF)] * 2 + [pltpu.SemaphoreType.DMA((4,))],
        compiler_params=pltpu.CompilerParams(vmem_limit_bytes=60 * 1024 * 1024),
    )(*outs)


def solution(mesh):
    return jax.shard_map(
        local,
        mesh=mesh,
        in_specs=(
            P(("row", "col"), None),
            P("row", "col", None, None, None),
            P("row", "col", None),
            P("row", "col"),
            P(),
            P(),
            P(("row", "col"), None),
        ),
        out_specs=(P(("row", "col"), None), P(("row", "col"), None), P(), P()),
        check_vma=False,
    )
```
